256 devices in a mesh: species: 16 (over z_hi, y, core), series: 16 (over z_lo, x).
Axes of the slice: x: 4, y: 4, z: 8 (z_hi: 2, z_lo: 4; z = z_hi * 4 + z_lo), core: 2. Of those that a mesh axis runs over, the one named last changes fastest.
Arguments:
- observed: bfloat16 [4096, 9216], P(('species', 'series')), may hold values from -6 to 6
- defocus: float32 [4096], P(('species', 'series')), may hold values from 1 to 4
- shift_center: int32 [2, 4096], P(None, ('species', 'series')), may hold values from -4 to 4
- pose_index: int32 [4096, 64], P(('species', 'series')), may hold values from 0 to 15
- pose_logprior: float32 [4096, 64], P(('species', 'series')), may hold values from -4 to 400
- reference_tiles: bfloat16 [512, 9216], P('species'), may hold values from -6 to 6
- series_id: int32 [4096], P(('species', 'series')), may hold values from 0 to 15
- tilt_id: int32 [4096], P(('species', 'series')), may hold values from 0 to 39
Outputs:
- item_loglik: float32 [4096], P(('species', 'series'))
- tilt_grads: float32 [3, 16, 40], P(None, 'series')
The draws below stay inside these ranges and needn't reach their ends.
All inputs are finite; a program needn't handle non-finite values.
Results may differ from the reference program's by a relative error of at most 0.012.
Values may be sent and summed in bfloat16 or wider, within the bound.
A program may use at most 128 MiB of HBM per device.

```python
import math
import jax
import jax.numpy as jnp
from jax import lax

BOX = 96
FREQ = 4608
SHIFT_Y = 8
SHIFT_X = 16
SPECIES = 32
POSES_SP = 16
POSE_K = 2
ITEMS_DEV = 16
ITEMS = 4096
TILTS = 40
SER_DEV = 1
SERIES = 16
N_SERIES = 16


def draw_pose_logprior(key, part):
    key = jax.random.fold_in(key, 11)
    pair_count = SPECIES * POSE_K
    subkeys = jax.random.split(key, 1)
    return jnp.clip(jax.random.normal(subkeys[0], (ITEMS, pair_count), jnp.float32), -4.0, 4.0)


def draw_series_id(key, part):
    key = jax.random.fold_in(key, 23)
    subkeys = jax.random.split(key, 3)
    position = jnp.arange(ITEMS, dtype=jnp.int32)
    owner_index = position // ITEMS_DEV % N_SERIES
    nearby = owner_index * SER_DEV + jax.random.randint(subkeys[0], (ITEMS,), 0, SER_DEV)
    anywhere = jax.random.randint(subkeys[1], (ITEMS,), 0, SERIES)
    staying = jax.random.randint(subkeys[2], (ITEMS,), 0, 4) < 3
    return jnp.where(staying, nearby, anywhere).astype(jnp.int32)


def place_ends(result, rng, smallest, largest):
    dims = result.shape
    place = [jax.random.randint(jax.random.fold_in(rng, axis), (), 0, dims[axis]) for axis in range(len(dims))]
    result = result.at[tuple(place)].set(smallest)
    longest = dims.index(max(dims))
    place[longest] = (place[longest] + 1) % dims[longest]
    return result.at[tuple(place)].set(largest)


def shard_levels(own_key, dims, pieces, smallest, largest):
    gain, own = 1.0, jax.random.fold_in(own_key, 6)
    for axis_at, shards_of in pieces:
        steps = jnp.exp(jax.random.uniform(jax.random.fold_in(own, axis_at), (shards_of,), jnp.float32, smallest / len(pieces), largest / len(pieces)))
        gain = gain * jnp.repeat(steps, dims[axis_at] // shards_of).reshape([-1 if axis == axis_at else 1 for axis in range(len(dims))])
    return gain


def centred(own_key, dims, deviation, most, shards=(), kind=jnp.bfloat16):
    entries = jax.random.normal(own_key, dims, jnp.float32) * deviation
    if len(shards) > 0:
        entries = shard_levels(own_key, dims, shards, -0.22, 0.18) * entries
    return jnp.clip(entries, min=-most, max=most).astype(kind)


def setup_inputs(seed: int = 0) -> dict:
    splits = jax.random.split(jax.random.key(seed), 9)
    return {
        "observed": centred(splits[0], (ITEMS, 2 * FREQ), 1.0, 6.0, ((0, 256),)),
        "defocus": jnp.clip(1.0 + 3.0 * jax.random.uniform(splits[1], (ITEMS,), jnp.float32) ** shard_levels(splits[1], (ITEMS,), ((0, 256),), -0.2, 0.2), 1.0, 4.0),
        "shift_center": place_ends(jax.random.randint(splits[2], (2, ITEMS), -4, 5), jax.random.fold_in(splits[2], 1), -4, 4).astype(jnp.int32),
        "pose_index": place_ends(jax.random.randint(splits[3], (ITEMS, SPECIES * POSE_K), 0, POSES_SP), jax.random.fold_in(splits[3], 1), 0, POSES_SP - 1).astype(jnp.int32),
        "pose_logprior": draw_pose_logprior(jax.random.fold_in(splits[8], 71), 0),
        "reference_tiles": centred(splits[5], (SPECIES * POSES_SP, 2 * FREQ), 1.0, 6.0, ((0, 16),)),
        "series_id": draw_series_id(jax.random.fold_in(splits[8], 71), 0),
        "tilt_id": place_ends(jax.random.randint(splits[7], (ITEMS,), 0, TILTS), jax.random.fold_in(splits[7], 1), 0, TILTS - 1).astype(jnp.int32),
    }


SCORE_SCALE = 0.03125
CTF_RATE = 4.0
AMP_PHASE = 0.1
ENV_RATE = 0.5
TWO_PI = 6.283185307179586


def freq_grid():
    half_box = BOX // 2
    flat_pos = jnp.arange(BOX * half_box, dtype=jnp.int32)
    row_pos = flat_pos // half_box
    col_pos = flat_pos % half_box
    freq_y = jnp.where(row_pos < half_box, row_pos, row_pos - BOX).astype(jnp.float32)
    freq_x = col_pos.astype(jnp.float32)
    return freq_y, freq_x


def phase_table():
    freq_y, freq_x = freq_grid()
    shift_pos = jnp.arange(SHIFT_Y * SHIFT_X, dtype=jnp.int32)
    delta_y = (shift_pos // SHIFT_X - SHIFT_Y // 2).astype(jnp.float32)
    delta_x = (shift_pos % SHIFT_X - SHIFT_X // 2).astype(jnp.float32)
    angles = (TWO_PI / BOX) * (freq_y[:, None] * delta_y[None, :] + freq_x[:, None] * delta_x[None, :])
    return jnp.concatenate([jnp.cos(angles), jnp.sin(angles)], 0).astype(jnp.bfloat16)


def shift_items(observed, shift_center):
    half_width = observed.shape[1] // 2
    freq_y, freq_x = freq_grid()
    center_y = shift_center[0].astype(jnp.float32)
    center_x = shift_center[1].astype(jnp.float32)
    angles = (TWO_PI / BOX) * (freq_y[None, :] * center_y[:, None] + freq_x[None, :] * center_x[:, None])
    cosine = jnp.cos(angles)
    sine_part = jnp.sin(angles)
    obs_re = observed[:, :half_width].astype(jnp.float32)
    obs_im = observed[:, half_width:].astype(jnp.float32)
    return jnp.concatenate([obs_re * cosine + obs_im * sine_part, obs_im * cosine - obs_re * sine_part], 1).astype(jnp.bfloat16)


def ctf_terms(defocus):
    freq_y, freq_x = freq_grid()
    half_box = BOX / 2.0
    radius_sq = (freq_y * freq_y + freq_x * freq_x) / (half_box * half_box)
    chi_phase = CTF_RATE * defocus[:, None] * radius_sq[None, :] - AMP_PHASE
    envelope = jnp.exp(-ENV_RATE * radius_sq)
    ctf_value = -jnp.sin(chi_phase) * envelope[None, :]
    ctf_slope = -jnp.cos(chi_phase) * (CTF_RATE * radius_sq * envelope)[None, :]
    return ctf_value, ctf_slope


def correlate(shifted, ctf_value, ctf_slope, chosen, phase_rows):
    half_width = shifted.shape[1] // 2
    freq_y, freq_x = freq_grid()
    obs_re = shifted[:, None, :half_width].astype(jnp.float32)
    obs_im = shifted[:, None, half_width:].astype(jnp.float32)
    ref_re = chosen[..., :half_width].astype(jnp.float32)
    ref_im = chosen[..., half_width:].astype(jnp.float32)
    prod_re = ref_re * obs_re + ref_im * obs_im
    prod_im = ref_re * obs_im - ref_im * obs_re
    value_b = ctf_value[:, None, :]
    slope_b = ctf_slope[:, None, :]
    ctf_x = value_b * (TWO_PI / BOX * freq_x)[None, None, :]
    ctf_y = value_b * (TWO_PI / BOX * freq_y)[None, None, :]
    filtered = jnp.stack([
        jnp.concatenate([value_b * prod_re, value_b * prod_im], -1),
        jnp.concatenate([slope_b * prod_re, slope_b * prod_im], -1),
        jnp.concatenate([ctf_x * prod_im, -(ctf_x * prod_re)], -1),
        jnp.concatenate([ctf_y * prod_im, -(ctf_y * prod_re)], -1)], 0).astype(jnp.bfloat16)
    flat_rows = filtered.reshape(-1, 2 * half_width)
    products = jnp.dot(flat_rows, phase_rows, preferred_element_type=jnp.float32)
    return products.reshape(4, shifted.shape[0], chosen.shape[1], phase_rows.shape[1])


def reference(observed, defocus, shift_center, pose_index, pose_logprior, reference_tiles, series_id, tilt_id):
    phase_rows = phase_table()
    shifted = shift_items(observed, shift_center)
    ctf_value, ctf_slope = ctf_terms(defocus)
    item_total = observed.shape[0]
    block_size = math.gcd(item_total, 256)
    block_count = item_total // block_size
    tiles_by_species = reference_tiles.reshape(SPECIES, POSES_SP, -1)

    def per_block(block_parts):
        part_shifted, part_value, part_slope, part_index, part_prior = block_parts

        def per_species(carried, species_at):
            tile_rows = tiles_by_species[species_at]
            chosen = jnp.take(tile_rows, part_index[:, species_at, :], axis=0)
            return carried, correlate(part_shifted, part_value, part_slope, chosen, phase_rows)

        unused, products = lax.scan(per_species, None, jnp.arange(SPECIES, dtype=jnp.int32))
        prior_t = jnp.transpose(part_prior, (1, 0, 2))
        scores = SCORE_SCALE * products[:, 0] + prior_t[..., None]
        highest = jnp.max(scores, axis=(0, 2, 3))
        weights = jnp.exp(scores - highest[None, :, None, None])
        totals = jnp.sum(weights, axis=(0, 2, 3))
        moments = SCORE_SCALE * jnp.sum(weights[:, None] * products[:, 1:], axis=(0, 3, 4))
        return highest + jnp.log(totals), moments / totals[None, :]

    loglik_blocks, grad_blocks = lax.map(per_block, (
        shifted.reshape(block_count, block_size, -1),
        ctf_value.reshape(block_count, block_size, -1),
        ctf_slope.reshape(block_count, block_size, -1),
        pose_index.reshape(block_count, block_size, SPECIES, POSE_K),
        pose_logprior.reshape(block_count, block_size, SPECIES, POSE_K)))
    item_loglik = loglik_blocks.reshape(item_total)
    gradients = jnp.transpose(grad_blocks, (1, 0, 2)).reshape(3, item_total)
    target = series_id * TILTS + tilt_id
    summed = jax.ops.segment_sum(gradients.T, target, num_segments=SERIES * TILTS)
    tilt_grads = summed.T.reshape(3, SERIES, TILTS)
    return item_loglik, tilt_grads
```

```python
import functools
import math

import jax
import jax.numpy as jnp
import ml_dtypes
import numpy as np
from jax import lax
from jax.experimental import pallas as pl
from jax.experimental.pallas import tpu as pltpu
from jax.sharding import PartitionSpec as P

MESH = pl.DeviceIdType.MESH
F32 = jnp.float32
BF16 = jnp.bfloat16

BOX = 96
FREQ = 4608
SHIFT_Y = 8
SHIFT_X = 16
POSES_SP = 16
TILTS = 40
SCORE_SCALE = 0.03125
CTF_RATE = 4.0
AMP_PHASE = 0.1
ENV_RATE = 0.5
TWO_PI = 6.283185307179586

GROUPS = 6
WIDTH = FREQ // GROUPS
SUB = 256
LANES = 128
ITEMS = 16
NY = 4
NX = 4
PAIRS = 8
ROWS = NY * PAIRS * ITEMS


def shift_halves():
    window = [(i - SHIFT_Y // 2, j - SHIFT_X // 2) for i in range(SHIFT_Y) for j in range(SHIFT_X)]
    inside = set(window)
    both = [s for s in window if s > (0, 0) and (-s[0], -s[1]) in inside]
    alone = [(0, 0)] + [s for s in window if (-s[0], -s[1]) not in inside]
    return both, alone


BOTH, ALONE = shift_halves()
N_BOTH, N_HALF = len(BOTH), len(BOTH) + len(ALONE)


def sine_fit():
    turn = np.cos(np.pi * (np.arange(400) + 0.5) / 400) * 0.5
    square = turn * turn
    odd = np.stack([turn * square**k for k in range(6)], 1)
    even = np.stack([square**k for k in range(7)], 1)
    sine = np.linalg.lstsq(odd, np.sin(2 * np.pi * turn), rcond=None)[0]
    cosine = np.linalg.lstsq(even, np.cos(2 * np.pi * turn), rcond=None)[0]
    return [float(np.float32(c)) for c in sine], [float(np.float32(c)) for c in cosine]


SINE, COSINE = sine_fit()


def sin_cos(turns):
    turn = turns - jnp.floor(turns + 0.5)
    square = turn * turn
    sine = SINE[-1]
    for c in SINE[-2::-1]:
        sine = sine * square + c
    cosine = COSINE[-1]
    for c in COSINE[-2::-1]:
        cosine = cosine * square + c
    return sine * turn, cosine


def frequencies():
    flat = np.arange(FREQ)
    row, col = flat // (BOX // 2), flat % (BOX // 2)
    return np.where(row < BOX // 2, row, row - BOX).astype(np.float64), col.astype(np.float64)


def frequency_rows():
    freq_y, freq_x = frequencies()
    k2 = (freq_y**2 + freq_x**2) / (BOX / 2.0) ** 2
    env = np.exp(-ENV_RATE * k2)
    rows = np.zeros((8, FREQ), np.float64)
    rows[0] = freq_y
    rows[1] = freq_x
    rows[2] = CTF_RATE * k2 / TWO_PI
    rows[3] = -env
    rows[4] = -CTF_RATE * k2 * env
    return rows.astype(np.float32)


def phase_tables():
    freq_y, freq_x = frequencies()
    half = np.array(BOTH + ALONE, np.float64)
    angle = TWO_PI / BOX * (freq_y[:, None] * half[None, :, 0] + freq_x[:, None] * half[None, :, 1])
    cosine, sine = np.cos(angle), np.sin(angle)
    rate_x, rate_y = (TWO_PI / BOX * freq_x)[:, None], (TWO_PI / BOX * freq_y)[:, None]
    table = np.zeros((2, FREQ, 3 * LANES), np.float64)
    for part, (value, slope) in enumerate(((cosine, -sine), (sine, cosine))):
        table[part, :, :N_HALF] = value
        table[part, :, N_HALF : N_HALF + N_BOTH] = rate_x * slope[:, :N_BOTH]
        table[part, :, LANES : LANES + N_HALF] = rate_y * slope
        table[part, :, LANES + N_HALF : LANES + 2 * N_HALF - N_BOTH] = rate_x * slope[:, N_BOTH:]
        table[part, :, 2 * LANES : 2 * LANES + N_HALF] = value
    table = table.reshape(2, GROUPS, WIDTH, 3 * LANES).transpose(1, 0, 2, 3)
    return table.astype(np.float32).astype(ml_dtypes.bfloat16)


def kernel(
    observed,
    reference_tiles,
    table_in,
    freq_rows,
    pose_index,
    pose_logprior,
    defocus,
    shift_center,
    series_id,
    tilt_id,
    loglik_out,
    tilt_out,
    raw,
    tiles,
    items,
    table,
    ext,
    priors,
    pose_hot,
    ctf,
    lhs,
    acc,
    acc_slope,
    part_out,
    part_in,
    series_out,
    series_in,
    species_out,
    species_in,
    local_sem,
    table_sem,
    item_send,
    item_recv,
    tile_send,
    tile_recv,
    ext_send,
    ext_recv,
    part_send,
    part_recv,
    series_send,
    series_recv,
    species_send,
    species_recv,
):
    sp = lax.axis_index("species")
    se = lax.axis_index("series")
    n_sp, n_se = species_in.shape[0], series_in.shape[0]
    z_hi, y, core = sp // 8, (sp // 2) % NY, sp % 2
    z_lo, x = se // NX, se % NX

    def at_y(other):
        return (z_hi * 8 + other * 2 + core, se)

    sibling = (z_hi * 8 + y * 2 + 1 - core, se)
    mirror = ((1 - z_hi) * 8 + y * 2 + core, (3 - z_lo) * NX + x)
    beside = (sp, z_lo * NX + x + 1 - 2 * (x % 2))
    y_next, y_prev, y_far = (y + 1) % NY, (y + 3) % NY, (y + 2) % NY
    y_from = (y + 3 + 2 * core) % NY
    y_to = (y + 1 + 2 * core) % NY
    own_tiles = z_hi * 2 + core
    own_far = (1 - z_hi) * 2 + core
    sibling_tiles = z_hi * 2 + 1 - core
    sibling_far = (1 - z_hi) * 2 + 1 - core

    raw_copy = pltpu.make_async_copy(observed, raw, local_sem.at[2 * GROUPS])
    raw_copy.start()

    def tile_copy(g, part):
        return pltpu.make_async_copy(
            reference_tiles.at[:, pl.ds(pl.multiple_of(part * FREQ + g * WIDTH, WIDTH), WIDTH)],
            tiles.at[g, own_tiles, part],
            local_sem.at[2 * g + part],
        )

    def table_copy(g):
        return pltpu.make_async_copy(table_in.at[g], table.at[g], table_sem.at[g])

    @pl.loop(0, GROUPS)
    def _(g):
        tile_copy(g, 0).start()
        tile_copy(g, 1).start()

    @pl.loop(0, GROUPS)
    def _(g):
        table_copy(g).start()

    barrier = pltpu.get_barrier_semaphore()

    @pl.loop(1, n_sp)
    def _(k):
        pl.semaphore_signal(barrier, inc=1, device_id=((sp + k) % n_sp, se), device_id_type=MESH)

    @pl.loop(1, n_se)
    def _(k):
        pl.semaphore_signal(barrier, inc=1, device_id=(sp, (se + k) % n_se), device_id_type=MESH)

    pl.semaphore_signal(barrier, inc=1, device_id=mirror, device_id_type=MESH)

    def remote(src, dst, send, recv, device):
        return pltpu.make_async_remote_copy(
            src_ref=src, dst_ref=dst, send_sem=send, recv_sem=recv, device_id=device, device_id_type=MESH
        )

    def send_item(kind, g, slot, device):
        ref = items.at[g, slot]
        return remote(ref, ref, item_send.at[kind, g], item_recv.at[kind, g], device)

    def send_tile(kind, lane, g, slot, device):
        ref = tiles.at[g, slot]
        return remote(ref, ref, tile_send.at[kind, g], tile_recv.at[lane, g], device)

    def send_ext(kind, device):
        ref = ext.at[y]
        return remote(ref, ref, ext_send.at[kind], ext_recv.at[kind], device)

    row16 = lax.broadcasted_iota(jnp.int32, (ITEMS, LANES), 0)
    lane16 = lax.broadcasted_iota(jnp.int32, (ITEMS, LANES), 1)

    def column(read):
        out = jnp.zeros((ITEMS, LANES), F32)
        for n in range(ITEMS):
            out = jnp.where(row16 == n, read(n).astype(F32), out)
        return out

    ext[y, :ITEMS, :] = jnp.concatenate([pose_index[...].astype(F32), pose_logprior[...]], 1)
    ext[y, ITEMS:, :] = column(lambda n: defocus[n])

    center_y = column(lambda n: shift_center[0, n])
    center_x = column(lambda n: shift_center[1, n])
    center_y = jnp.concatenate([center_y, center_y], 1)
    center_x = jnp.concatenate([center_x, center_x], 1)
    raw_copy.wait()

    @pl.loop(0, GROUPS)
    def _(g):
        for sub in range(WIDTH // SUB):
            at = g * WIDTH + sub * SUB
            re_cols = pl.ds(pl.multiple_of(at, SUB), SUB)
            im_cols = pl.ds(pl.multiple_of(FREQ + at, SUB), SUB)
            turns = freq_rows[0:1, re_cols] * center_y + freq_rows[1:2, re_cols] * center_x
            sine, cosine = sin_cos(turns * (1.0 / BOX))
            re, im = raw[:, re_cols].astype(F32), raw[:, im_cols].astype(F32)
            cols = slice(sub * SUB, (sub + 1) * SUB)
            items[g, y, 0, :, cols] = (re * cosine + im * sine).astype(BF16)
            items[g, y, 1, :, cols] = (im * cosine - re * sine).astype(BF16)

    pl.semaphore_wait(barrier, n_sp + n_se - 1)

    send_ext(0, at_y(y_next)).start()
    send_ext(1, at_y(y_prev)).start()
    send_ext(2, at_y(y_far)).start()

    @pl.loop(0, GROUPS)
    def _(g):
        send_item(0, g, y, at_y(y_next)).start()
        send_item(1, g, y, at_y(y_prev)).start()
        tile_copy(g, 0).wait()
        tile_copy(g, 1).wait()

        @pl.when(g % 2 == x % 2)
        def _():
            send_tile(1, 1, g, own_tiles, mirror).start()

        send_tile(0, 0, g, own_tiles, sibling).start()

    acc[...] = jnp.zeros_like(acc)
    acc_slope[...] = jnp.zeros_like(acc_slope)

    send_ext(0, at_y(y_next)).wait_recv()
    send_ext(1, at_y(y_prev)).wait_recv()
    send_ext(2, at_y(y_far)).wait_recv()

    lane_f = lane16.astype(F32)
    to_front = (LANES - 8 * y) % LANES

    @pl.loop(0, NY)
    def _(b):
        moved = pltpu.roll(ext[b, :ITEMS, :], to_front, 1)
        priors[b] = moved
        for h in range(2):
            for j in range(PAIRS):
                pose = moved[:, 32 * h + j : 32 * h + j + 1] + float((j // 2) * POSES_SP)
                hot = jnp.where(lane_f == pose, 1.0, 0.0)[:, : 4 * POSES_SP]
                pose_hot[h, b, j * ITEMS : (j + 1) * ITEMS, :] = hot.astype(BF16)

    @pl.loop(0, NY)
    def _(b):
        focus = ext[b, ITEMS:, :]
        focus = jnp.concatenate([focus, focus], 1)

        @pl.loop(0, FREQ // SUB)
        def _(c):
            cols = pl.ds(pl.multiple_of(c * SUB, SUB), SUB)
            turns = focus * freq_rows[2:3, cols] - AMP_PHASE / TWO_PI
            sine, cosine = sin_cos(turns)
            ctf[0, b, :, cols] = (sine * freq_rows[3:4, cols]).astype(BF16)
            ctf[1, b, :, cols] = (cosine * freq_rows[4:5, cols]).astype(BF16)

    def pass_items(g):
        send_item(core, g, y_from, at_y(y_from)).wait_recv()
        send_item(2, g, y_from, at_y(y_to)).start()

    def pass_tiles(g):
        send_tile(1, 1, g, own_far, mirror).wait_recv()

        @pl.when(g % 2 == x % 2)
        def _():
            send_tile(2, 1, g, own_far, beside).start()

        send_tile(3, 2, g, own_far, sibling).start()

    pass_items(0)

    @pl.loop(0, 2 * GROUPS)
    def _(i):
        far = jnp.where(i < 3, 0, jnp.where(i >= 10, 1, i % 2))
        g = jnp.where(i < 3, i, jnp.where(i >= 10, i - 6, jnp.where(i % 2 == 1, (i - 3) // 2, i // 2 + 1)))
        h = (z_hi + far) % 2

        @pl.when(far == 0)
        def _():
            send_item(1 - core, g, y_to, at_y(y_to)).wait_recv()
            send_item(2, g, y_far, at_y(y_to)).wait_recv()
            send_tile(0, 0, g, sibling_tiles, sibling).wait_recv()
            table_copy(g).wait()

        @pl.when(far == 1)
        def _():
            send_tile(3, 2, g, sibling_far, sibling).wait_recv()

        for sub in range(WIDTH // SUB):
            cols = slice(sub * SUB, (sub + 1) * SUB)
            tile_re = tiles[g, pl.ds(2 * h, 2), 0, :, cols].reshape(4 * POSES_SP, SUB)
            tile_im = tiles[g, pl.ds(2 * h, 2), 1, :, cols].reshape(4 * POSES_SP, SUB)
            freqs = pl.ds(pl.multiple_of(g * WIDTH + sub * SUB, SUB), SUB)
            for b in range(NY):
                hot = pose_hot[h, b]
                re = jnp.dot(hot, tile_re, preferred_element_type=F32).reshape(PAIRS, ITEMS, SUB).astype(BF16)
                im = jnp.dot(hot, tile_im, preferred_element_type=F32).reshape(PAIRS, ITEMS, SUB).astype(BF16)
                value, slope = ctf[0, b, :, freqs], ctf[1, b, :, freqs]
                o_re, o_im = items[g, b, 0, :, cols], items[g, b, 1, :, cols]
                prod_re = re * o_re + im * o_im
                prod_im = re * o_im - im * o_re
                rows = slice(b * PAIRS * ITEMS, (b + 1) * PAIRS * ITEMS)
                for q, part in enumerate((prod_re * value, prod_im * value, prod_re * slope, prod_im * slope)):
                    lhs[q, rows, cols] = part.reshape(PAIRS * ITEMS, SUB)
        for q in range(2):
            acc[h, q] += jnp.dot(lhs[q], table[g, q, :, : 2 * LANES], preferred_element_type=F32)
            acc_slope[h, q] += jnp.dot(lhs[2 + q], table[g, q, :, 2 * LANES :], preferred_element_type=F32)

        @pl.when((far == 0) & (g < GROUPS - 1))
        def _():
            pass_items(g + 1)

        @pl.when((i >= 2) & (i < 10) & (i % 2 == 0))
        def _():
            pass_tiles((i - 2) // 2)

        @pl.when(i >= 9)
        def _():
            @pl.when(i < 11)
            def _():
                pass_tiles(i - 5)

    plus_ok, minus_ok = lane16 < N_HALF, lane16 < N_BOTH
    lowest = -1e30

    @pl.loop(0, NY)
    def _(b):
        message = priors[b]
        places = []
        for h in range(2):
            for j in range(PAIRS):
                places.append((h, j, pl.ds(pl.multiple_of((b * PAIRS + j) * ITEMS, ITEMS), ITEMS)))
        scores = []
        for h, j, rows in places:
            prior = message[:, 64 + 32 * h + j : 64 + 32 * h + j + 1]
            re, im = acc[h, 0, rows, :LANES], acc[h, 1, rows, :LANES]
            scores.append(
                (
                    jnp.where(plus_ok, SCORE_SCALE * (re + im) + prior, lowest),
                    jnp.where(minus_ok, SCORE_SCALE * (re - im) + prior, lowest),
                )
            )
        top = functools.reduce(jnp.maximum, [jnp.maximum(p, m) for p, m in scores])
        top = jnp.max(top, axis=1, keepdims=True)
        zero = jnp.zeros((ITEMS, LANES), F32)
        total, d_focus, d_x, d_x_alone, d_y = zero, zero, zero, zero, zero
        for (h, j, rows), (p, m) in zip(places, scores):
            p, m = jnp.exp(p - top), jnp.exp(m - top)
            total += p + m
            re, im = acc_slope[h, 0, rows, :], acc_slope[h, 1, rows, :]
            d_focus += p * (re + im) + m * (re - im)
            re, im = acc[h, 0, rows, :LANES], acc[h, 1, rows, :LANES]
            d_x += pltpu.roll(p, N_HALF, 1) * (re + im) - pltpu.roll(m, N_HALF, 1) * (re - im)
            re, im = acc[h, 0, rows, LANES:], acc[h, 1, rows, LANES:]
            d_y += p * (re + im) - m * (re - im)
            d_x_alone += pltpu.roll(p, N_HALF - N_BOTH, 1) * (re + im)
        d_x = jnp.where(lane16 >= N_HALF, d_x, 0.0)
        d_x += jnp.where((lane16 >= N_HALF) & (lane16 < 2 * N_HALF - N_BOTH), d_x_alone, 0.0)
        out = jnp.where(lane16 == 0, top, 0.0)
        for at, term in enumerate((total, d_focus, d_x, d_y)):
            out = jnp.where(lane16 == at + 1, jnp.sum(term, axis=1, keepdims=True), out)
        part_out[b] = out

    def send_part(k):
        other = (y + k) % NY
        return remote(part_out.at[other], part_in.at[y], part_send.at[k], part_recv.at[k], at_y(other))

    for k in range(1, NY):
        send_part(k).start()
    part_in[y] = part_out[y]
    for k in range(1, NY):
        other = (y + NY - k) % NY
        remote(part_out.at[y], part_in.at[other], part_send.at[k], part_recv.at[k], at_y(other)).wait_recv()

    tops = [part_in[b, :, 0:1] for b in range(NY)]
    top = functools.reduce(jnp.maximum, tops)
    keeps = [jnp.exp(t - top) for t in tops]
    sums = [sum(part_in[b, :, at : at + 1] * keeps[b] for b in range(NY)) for at in range(1, 5)]
    loglik = top + jnp.log(sums[0])
    grads = [s * SCORE_SCALE / sums[0] for s in sums[1:]]
    loglik_out[...] = jnp.sum(jnp.where(row16 == lane16, loglik, 0.0), axis=0, keepdims=True) + jnp.zeros((8, LANES), F32)

    tilt = column(lambda n: tilt_id[n])
    placed = jnp.zeros((ITEMS, LANES), F32)
    for at, grad in enumerate(grads):
        placed = jnp.where(lane_f == tilt + float(at * TILTS), grad, placed)
    sums_by_series = jnp.zeros((n_se, LANES), F32)
    series_row = lax.broadcasted_iota(jnp.int32, (n_se, LANES), 0)
    for n in range(ITEMS):
        sums_by_series += jnp.where(series_row == series_id[n], placed[n : n + 1, :], 0.0)
    for s in range(n_se):
        series_out[s] = sums_by_series[s : s + 1, :]

    def send_series(k):
        other = (se + k) % n_se
        return remote(series_out.at[other], series_in.at[se], series_send.at[k], series_recv.at[k], (sp, other))

    def take_series(k):
        other = (se + n_se - k) % n_se
        return remote(series_out.at[se], series_in.at[other], series_send.at[k], series_recv.at[k], (sp, other))

    @pl.loop(1, n_se)
    def _(k):
        send_series(k).start()

    series_in[se] = series_out[se]

    @pl.loop(1, n_se)
    def _(k):
        take_series(k).wait_recv()

    species_out[...] = sum(series_in[s] for s in range(n_se))

    def send_species(k):
        other = (sp + k) % n_sp
        return remote(species_out, species_in.at[sp], species_send.at[k], species_recv.at[k], (other, se))

    def take_species(k):
        other = (sp + n_sp - k) % n_sp
        return remote(species_out, species_in.at[other], species_send.at[k], species_recv.at[k], (other, se))

    @pl.loop(1, n_sp)
    def _(k):
        send_species(k).start()

    species_in[sp] = species_out[...]

    @pl.loop(1, n_sp)
    def _(k):
        take_species(k).wait_recv()

    tilt_out[...] = sum(species_in[s] for s in range(n_sp)) + jnp.zeros((8, LANES), F32)

    send_ext(0, at_y(y_next)).wait_send()
    send_ext(1, at_y(y_prev)).wait_send()
    send_ext(2, at_y(y_far)).wait_send()

    @pl.loop(0, GROUPS)
    def _(g):
        send_item(0, g, y, at_y(y_next)).wait_send()
        send_item(1, g, y, at_y(y_prev)).wait_send()
        send_item(2, g, y_from, at_y(y_to)).wait_send()
        send_tile(0, 0, g, own_tiles, sibling).wait_send()
        send_tile(3, 2, g, own_far, sibling).wait_send()

        @pl.when(g % 2 == x % 2)
        def _():
            send_tile(1, 1, g, own_tiles, mirror).wait_send()
            send_tile(2, 1, g, own_far, beside).wait_send()

    for k in range(1, NY):
        send_part(k).wait_send()

    @pl.loop(1, n_se)
    def _(k):
        send_series(k).wait_send()

    @pl.loop(1, n_sp)
    def _(k):
        send_species(k).wait_send()


def solution(mesh):
    n_sp, n_se = mesh.shape["species"], mesh.shape["series"]
    placed = (
        P(("species", "series"), None),
        P(("species", "series")),
        P(None, ("species", "series")),
        P(("species", "series"), None),
        P(("species", "series"), None),
        P("species", None),
        P(("species", "series")),
        P(("species", "series")),
    )
    table = phase_tables()
    rows = frequency_rows()
    any_space = pl.BlockSpec(memory_space=pl.ANY)
    vmem = pl.BlockSpec(memory_space=pltpu.VMEM)
    smem = pl.BlockSpec(memory_space=pltpu.SMEM)
    dma = pltpu.SemaphoreType.DMA

    def body(observed, defocus, shift_center, pose_index, pose_logprior, reference_tiles, series_id, tilt_id):
        loglik, tilts = pl.pallas_call(
            kernel,
            out_shape=(jax.ShapeDtypeStruct((8, LANES), F32), jax.ShapeDtypeStruct((8, LANES), F32)),
            in_specs=[any_space, any_space, any_space, vmem, vmem, vmem, smem, smem, smem, smem],
            out_specs=(vmem, vmem),
            scratch_shapes=[
                pltpu.VMEM((ITEMS, 2 * FREQ), BF16),
                pltpu.VMEM((GROUPS, 4, 2, 2 * POSES_SP, WIDTH), BF16),
                pltpu.VMEM((GROUPS, NY, 2, ITEMS, WIDTH), BF16),
                pltpu.VMEM((GROUPS, 2, WIDTH, 3 * LANES), BF16),
                pltpu.VMEM((NY, 2 * ITEMS, LANES), F32),
                pltpu.VMEM((NY, ITEMS, LANES), F32),
                pltpu.VMEM((2, NY, PAIRS * ITEMS, 4 * POSES_SP), BF16),
                pltpu.VMEM((2, NY, ITEMS, FREQ), BF16),
                pltpu.VMEM((4, ROWS, WIDTH), BF16),
                pltpu.VMEM((2, 2, ROWS, 2 * LANES), F32),
                pltpu.VMEM((2, 2, ROWS, LANES), F32),
                pltpu.VMEM((NY, ITEMS, LANES), F32),
                pltpu.VMEM((NY, ITEMS, LANES), F32),
                pltpu.VMEM((n_se, 1, LANES), F32),
                pltpu.VMEM((n_se, 1, LANES), F32),
                pltpu.VMEM((1, LANES), F32),
                pltpu.VMEM((n_sp, 1, LANES), F32),
                dma((2 * GROUPS + 1,)),
                dma((GROUPS,)),
                dma((3, GROUPS)),
                dma((3, GROUPS)),
                dma((4, GROUPS)),
                dma((3, GROUPS)),
                dma((3,)),
                dma((3,)),
                dma((NY,)),
                dma((NY,)),
                dma((n_se,)),
                dma((n_se,)),
                dma((n_sp,)),
                dma((n_sp,)),
            ],
            compiler_params=pltpu.CompilerParams(
                collective_id=0, has_side_effects=True, vmem_limit_bytes=60 * 2**20
            ),
        )(
            observed,
            reference_tiles,
            jnp.asarray(table),
            jnp.asarray(rows),
            pose_index,
            pose_logprior,
            defocus,
            shift_center,
            series_id,
            tilt_id,
        )
        tilt_grads = tilts[0, : 3 * TILTS].reshape(3, 1, TILTS)
        return loglik[0, :ITEMS], tilt_grads

    return jax.shard_map(
        body,
        mesh=mesh,
        in_specs=placed,
        out_specs=(P(("species", "series")), P(None, "series", None)),
        check_vma=False,
    )
```

```python
import functools
import math

import jax
import jax.numpy as jnp
import ml_dtypes
import numpy as np
from jax import lax
from jax.experimental import pallas as pl
from jax.experimental.pallas import tpu as pltpu
from jax.sharding import PartitionSpec as P

MESH = pl.DeviceIdType.MESH
F32 = jnp.float32
BF16 = jnp.bfloat16

BOX = 96
FREQ = 4608
SHIFT_Y = 8
SHIFT_X = 16
POSES_SP = 16
TILTS = 40
SCORE_SCALE = 0.03125
CTF_RATE = 4.0
AMP_PHASE = 0.1
ENV_RATE = 0.5
TWO_PI = 6.283185307179586

GROUPS = 6
WIDTH = FREQ // GROUPS
SUB = 256
LANES = 128
ITEMS = 16
NY = 4
NX = 4
PAIRS = 8
ROWS = NY * PAIRS * ITEMS


def shift_halves():
    window = [(i - SHIFT_Y // 2, j - SHIFT_X // 2) for i in range(SHIFT_Y) for j in range(SHIFT_X)]
    inside = set(window)
    both = [s for s in window if s > (0, 0) and (-s[0], -s[1]) in inside]
    alone = [(0, 0)] + [s for s in window if (-s[0], -s[1]) not in inside]
    return both, alone


BOTH, ALONE = shift_halves()
N_BOTH, N_HALF = len(BOTH), len(BOTH) + len(ALONE)


def sine_fit():
    turn = np.cos(np.pi * (np.arange(400) + 0.5) / 400) * 0.5
    square = turn * turn
    odd = np.stack([turn * square**k for k in range(6)], 1)
    even = np.stack([square**k for k in range(7)], 1)
    sine = np.linalg.lstsq(odd, np.sin(2 * np.pi * turn), rcond=None)[0]
    cosine = np.linalg.lstsq(even, np.cos(2 * np.pi * turn), rcond=None)[0]
    return [float(np.float32(c)) for c in sine], [float(np.float32(c)) for c in cosine]


SINE, COSINE = sine_fit()


def sin_cos(turns):
    turn = turns - jnp.floor(turns + 0.5)
    square = turn * turn
    sine = SINE[-1]
    for c in SINE[-2::-1]:
        sine = sine * square + c
    cosine = COSINE[-1]
    for c in COSINE[-2::-1]:
        cosine = cosine * square + c
    return sine * turn, cosine


def frequencies():
    flat = np.arange(FREQ)
    row, col = flat // (BOX // 2), flat % (BOX // 2)
    return np.where(row < BOX // 2, row, row - BOX).astype(np.float64), col.astype(np.float64)


def frequency_rows():
    freq_y, freq_x = frequencies()
    k2 = (freq_y**2 + freq_x**2) / (BOX / 2.0) ** 2
    env = np.exp(-ENV_RATE * k2)
    rows = np.zeros((8, FREQ), np.float64)
    rows[0] = freq_y
    rows[1] = freq_x
    rows[2] = CTF_RATE * k2 / TWO_PI
    rows[3] = -env
    rows[4] = -CTF_RATE * k2 * env
    return rows.astype(np.float32)


def phase_tables():
    freq_y, freq_x = frequencies()
    half = np.array(BOTH + ALONE, np.float64)
    angle = TWO_PI / BOX * (freq_y[:, None] * half[None, :, 0] + freq_x[:, None] * half[None, :, 1])
    cosine, sine = np.cos(angle), np.sin(angle)
    rate_x, rate_y = (TWO_PI / BOX * freq_x)[:, None], (TWO_PI / BOX * freq_y)[:, None]
    table = np.zeros((2, FREQ, 3 * LANES), np.float64)
    for part, (value, slope) in enumerate(((cosine, -sine), (sine, cosine))):
        table[part, :, :N_HALF] = value
        table[part, :, N_HALF : N_HALF + N_BOTH] = rate_x * slope[:, :N_BOTH]
        table[part, :, LANES : LANES + N_HALF] = rate_y * slope
        table[part, :, LANES + N_HALF : LANES + 2 * N_HALF - N_BOTH] = rate_x * slope[:, N_BOTH:]
        table[part, :, 2 * LANES : 2 * LANES + N_HALF] = value
    table = table.reshape(2, GROUPS, WIDTH, 3 * LANES).transpose(1, 0, 2, 3)
    return table.astype(np.float32).astype(ml_dtypes.bfloat16)


def kernel(
    observed,
    reference_tiles,
    table_in,
    freq_rows,
    pose_index,
    pose_logprior,
    defocus,
    shift_center,
    series_id,
    tilt_id,
    loglik_out,
    tilt_out,
    raw,
    tiles,
    items,
    table,
    ext,
    priors,
    pose_hot,
    ctf,
    lhs,
    acc,
    acc_slope,
    part_out,
    part_in,
    series_out,
    series_in,
    species_out,
    species_in,
    local_sem,
    table_sem,
    item_send,
    item_recv,
    tile_send,
    tile_recv,
    ext_send,
    ext_recv,
    part_send,
    part_recv,
    series_send,
    series_recv,
    species_send,
    species_recv,
):
    sp = lax.axis_index("species")
    se = lax.axis_index("series")
    n_sp, n_se = species_in.shape[0], series_in.shape[0]
    z_hi, y, core = sp // 8, (sp // 2) % NY, sp % 2
    z_lo, x = se // NX, se % NX

    def at_y(other):
        return (z_hi * 8 + other * 2 + core, se)

    sibling = (z_hi * 8 + y * 2 + 1 - core, se)
    mirror = ((1 - z_hi) * 8 + y * 2 + core, (3 - z_lo) * NX + x)
    beside = (sp, z_lo * NX + x + 1 - 2 * (x % 2))
    own_tiles = z_hi * 2 + core
    own_far = (1 - z_hi) * 2 + core
    sibling_tiles = z_hi * 2 + 1 - core
    sibling_far = (1 - z_hi) * 2 + 1 - core

    raw_copy = pltpu.make_async_copy(observed, raw, local_sem.at[2 * GROUPS])
    raw_copy.start()

    def tile_copy(g, part):
        return pltpu.make_async_copy(
            reference_tiles.at[:, pl.ds(pl.multiple_of(part * FREQ + g * WIDTH, WIDTH), WIDTH)],
            tiles.at[g, own_tiles, part],
            local_sem.at[2 * g + part],
        )

    def table_copy(g):
        return pltpu.make_async_copy(table_in.at[g], table.at[g], table_sem.at[g])

    @pl.loop(0, GROUPS)
    def _(g):
        tile_copy(g, 0).start()
        tile_copy(g, 1).start()

    @pl.loop(0, GROUPS)
    def _(g):
        table_copy(g).start()

    barrier = pltpu.get_barrier_semaphore()

    @pl.loop(1, n_sp)
    def _(k):
        pl.semaphore_signal(barrier, inc=1, device_id=((sp + k) % n_sp, se), device_id_type=MESH)

    @pl.loop(1, n_se)
    def _(k):
        pl.semaphore_signal(barrier, inc=1, device_id=(sp, (se + k) % n_se), device_id_type=MESH)

    pl.semaphore_signal(barrier, inc=1, device_id=mirror, device_id_type=MESH)

    def remote(src, dst, send, recv, device):
        return pltpu.make_async_remote_copy(
            src_ref=src, dst_ref=dst, send_sem=send, recv_sem=recv, device_id=device, device_id_type=MESH
        )

    def send_item(k, g):
        ref = items.at[g, y]
        return remote(ref, ref, item_send.at[k, g], item_recv.at[k, g], at_y((y + k) % NY))

    def take_item(k, g):
        other = (y + NY - k) % NY
        ref = items.at[g, other]
        return remote(ref, ref, item_send.at[k, g], item_recv.at[k, g], at_y(other))

    def send_tile(kind, lane, g, slot, device):
        ref = tiles.at[g, slot]
        return remote(ref, ref, tile_send.at[kind, g], tile_recv.at[lane, g], device)

    def send_ext(k):
        ref = ext.at[y]
        return remote(ref, ref, ext_send.at[k], ext_recv.at[k], at_y((y + k) % NY))

    def take_ext(k):
        other = (y + NY - k) % NY
        ref = ext.at[other]
        return remote(ref, ref, ext_send.at[k], ext_recv.at[k], at_y(other))

    row16 = lax.broadcasted_iota(jnp.int32, (ITEMS, LANES), 0)
    lane16 = lax.broadcasted_iota(jnp.int32, (ITEMS, LANES), 1)

    def column(read):
        out = jnp.zeros((ITEMS, LANES), F32)
        for n in range(ITEMS):
            out = jnp.where(row16 == n, read(n).astype(F32), out)
        return out

    ext[y, :ITEMS, :] = jnp.concatenate([pose_index[...].astype(F32), pose_logprior[...]], 1)
    ext[y, ITEMS:, :] = column(lambda n: defocus[n])

    center_y = column(lambda n: shift_center[0, n])
    center_x = column(lambda n: shift_center[1, n])
    center_y = jnp.concatenate([center_y, center_y], 1)
    center_x = jnp.concatenate([center_x, center_x], 1)
    pl.semaphore_wait(barrier, n_sp + n_se - 1)

    for k in range(1, NY):
        send_ext(k).start()
    raw_copy.wait()

    @pl.loop(0, GROUPS)
    def _(g):
        for sub in range(WIDTH // SUB):
            at = g * WIDTH + sub * SUB
            re_cols = pl.ds(pl.multiple_of(at, SUB), SUB)
            im_cols = pl.ds(pl.multiple_of(FREQ + at, SUB), SUB)
            turns = freq_rows[0:1, re_cols] * center_y + freq_rows[1:2, re_cols] * center_x
            sine, cosine = sin_cos(turns * (1.0 / BOX))
            re, im = raw[:, re_cols].astype(F32), raw[:, im_cols].astype(F32)
            cols = slice(sub * SUB, (sub + 1) * SUB)
            items[g, y, 0, :, cols] = (re * cosine + im * sine).astype(BF16)
            items[g, y, 1, :, cols] = (im * cosine - re * sine).astype(BF16)
        for k in range(1, NY):
            send_item(k, g).start()
        tile_copy(g, 0).wait()
        tile_copy(g, 1).wait()

        @pl.when(g % 2 == x % 2)
        def _():
            send_tile(1, 1, g, own_tiles, mirror).start()

        send_tile(0, 0, g, own_tiles, sibling).start()

    acc[...] = jnp.zeros_like(acc)
    acc_slope[...] = jnp.zeros_like(acc_slope)

    for k in range(1, NY):
        take_ext(k).wait_recv()

    lane_f = lane16.astype(F32)
    to_front = (LANES - 8 * y) % LANES

    @pl.loop(0, NY)
    def _(b):
        moved = pltpu.roll(ext[b, :ITEMS, :], to_front, 1)
        priors[b] = moved
        for h in range(2):
            for j in range(PAIRS):
                pose = moved[:, 32 * h + j : 32 * h + j + 1] + float((j // 2) * POSES_SP)
                hot = jnp.where(lane_f == pose, 1.0, 0.0)[:, : 4 * POSES_SP]
                pose_hot[h, b, j * ITEMS : (j + 1) * ITEMS, :] = hot.astype(BF16)

    @pl.loop(0, NY)
    def _(b):
        focus = ext[b, ITEMS:, :]
        focus = jnp.concatenate([focus, focus], 1)

        @pl.loop(0, FREQ // SUB)
        def _(c):
            cols = pl.ds(pl.multiple_of(c * SUB, SUB), SUB)
            turns = focus * freq_rows[2:3, cols] - AMP_PHASE / TWO_PI
            sine, cosine = sin_cos(turns)
            ctf[0, b, :, cols] = (sine * freq_rows[3:4, cols]).astype(BF16)
            ctf[1, b, :, cols] = (cosine * freq_rows[4:5, cols]).astype(BF16)

    def pass_own(g):
        send_tile(1, 1, g, own_far, mirror).wait_recv()
        send_tile(2, 1, g, own_far, beside).start()
        send_tile(3, 2, g, own_far, sibling).start()

    def pass_other(g):
        send_tile(2, 1, g, own_far, beside).wait_recv()
        send_tile(3, 2, g, own_far, sibling).start()

    @pl.loop(0, 2 * GROUPS)
    def _(i):
        far = jnp.where(i < 5, 0, jnp.where(i == 6, 0, 1))
        g = jnp.where(i < 5, i, jnp.where(i == 5, 0, jnp.where(i == 6, 5, i - 6)))
        h = (z_hi + far) % 2

        @pl.when(far == 0)
        def _():
            for k in range(1, NY):
                take_item(k, g).wait_recv()
            send_tile(0, 0, g, sibling_tiles, sibling).wait_recv()
            table_copy(g).wait()

        @pl.when(far == 1)
        def _():
            send_tile(3, 2, g, sibling_far, sibling).wait_recv()

        for sub in range(WIDTH // SUB):
            cols = slice(sub * SUB, (sub + 1) * SUB)
            tile_re = tiles[g, pl.ds(2 * h, 2), 0, :, cols].reshape(4 * POSES_SP, SUB)
            tile_im = tiles[g, pl.ds(2 * h, 2), 1, :, cols].reshape(4 * POSES_SP, SUB)
            freqs = pl.ds(pl.multiple_of(g * WIDTH + sub * SUB, SUB), SUB)
            for b in range(NY):
                hot = pose_hot[h, b]
                re = jnp.dot(hot, tile_re, preferred_element_type=F32).reshape(PAIRS, ITEMS, SUB).astype(BF16)
                im = jnp.dot(hot, tile_im, preferred_element_type=F32).reshape(PAIRS, ITEMS, SUB).astype(BF16)
                value, slope = ctf[0, b, :, freqs], ctf[1, b, :, freqs]
                o_re, o_im = items[g, b, 0, :, cols], items[g, b, 1, :, cols]
                prod_re = re * o_re + im * o_im
                prod_im = re * o_im - im * o_re
                rows = slice(b * PAIRS * ITEMS, (b + 1) * PAIRS * ITEMS)
                for q, part in enumerate((prod_re * value, prod_im * value, prod_re * slope, prod_im * slope)):
                    lhs[q, rows, cols] = part.reshape(PAIRS * ITEMS, SUB)
        for q in range(2):
            acc[h, q] += jnp.dot(lhs[q], table[g, q, :, : 2 * LANES], preferred_element_type=F32)
            acc_slope[h, q] += jnp.dot(lhs[2 + q], table[g, q, :, 2 * LANES :], preferred_element_type=F32)

        for at, k, own in ((0, 0, True), (2, 1, True), (3, 0, False), (4, 2, True), (5, 1, False), (7, 2, False)):

            @pl.when(i == at)
            def _(k=k, own=own):
                if own:
                    pass_own(2 * k + x % 2)
                else:
                    pass_other(2 * k + 1 - x % 2)

    plus_ok, minus_ok = lane16 < N_HALF, lane16 < N_BOTH
    lowest = -1e30

    @pl.loop(0, NY)
    def _(b):
        message = priors[b]
        places = []
        for h in range(2):
            for j in range(PAIRS):
                places.append((h, j, pl.ds(pl.multiple_of((b * PAIRS + j) * ITEMS, ITEMS), ITEMS)))
        scores = []
        for h, j, rows in places:
            prior = message[:, 64 + 32 * h + j : 64 + 32 * h + j + 1]
            re, im = acc[h, 0, rows, :LANES], acc[h, 1, rows, :LANES]
            scores.append(
                (
                    jnp.where(plus_ok, SCORE_SCALE * (re + im) + prior, lowest),
                    jnp.where(minus_ok, SCORE_SCALE * (re - im) + prior, lowest),
                )
            )
        top = functools.reduce(jnp.maximum, [jnp.maximum(p, m) for p, m in scores])
        top = jnp.max(top, axis=1, keepdims=True)
        zero = jnp.zeros((ITEMS, LANES), F32)
        total, d_focus, d_x, d_x_alone, d_y = zero, zero, zero, zero, zero
        for (h, j, rows), (p, m) in zip(places, scores):
            p, m = jnp.exp(p - top), jnp.exp(m - top)
            total += p + m
            re, im = acc_slope[h, 0, rows, :], acc_slope[h, 1, rows, :]
            d_focus += p * (re + im) + m * (re - im)
            re, im = acc[h, 0, rows, :LANES], acc[h, 1, rows, :LANES]
            d_x += pltpu.roll(p, N_HALF, 1) * (re + im) - pltpu.roll(m, N_HALF, 1) * (re - im)
            re, im = acc[h, 0, rows, LANES:], acc[h, 1, rows, LANES:]
            d_y += p * (re + im) - m * (re - im)
            d_x_alone += pltpu.roll(p, N_HALF - N_BOTH, 1) * (re + im)
        d_x = jnp.where(lane16 >= N_HALF, d_x, 0.0)
        d_x += jnp.where((lane16 >= N_HALF) & (lane16 < 2 * N_HALF - N_BOTH), d_x_alone, 0.0)
        out = jnp.where(lane16 == 0, top, 0.0)
        for at, term in enumerate((total, d_focus, d_x, d_y)):
            out = jnp.where(lane16 == at + 1, jnp.sum(term, axis=1, keepdims=True), out)
        part_out[b] = out

    def send_part(k):
        other = (y + k) % NY
        return remote(part_out.at[other], part_in.at[y], part_send.at[k], part_recv.at[k], at_y(other))

    for k in range(1, NY):
        send_part(k).start()
    part_in[y] = part_out[y]
    for k in range(1, NY):
        other = (y + NY - k) % NY
        remote(part_out.at[y], part_in.at[other], part_send.at[k], part_recv.at[k], at_y(other)).wait_recv()

    tops = [part_in[b, :, 0:1] for b in range(NY)]
    top = functools.reduce(jnp.maximum, tops)
    keeps = [jnp.exp(t - top) for t in tops]
    sums = [sum(part_in[b, :, at : at + 1] * keeps[b] for b in range(NY)) for at in range(1, 5)]
    loglik = top + jnp.log(sums[0])
    grads = [s * SCORE_SCALE / sums[0] for s in sums[1:]]
    loglik_out[...] = jnp.sum(jnp.where(row16 == lane16, loglik, 0.0), axis=0)[:ITEMS]

    tilt = column(lambda n: tilt_id[n])
    placed = jnp.zeros((ITEMS, LANES), F32)
    for at, grad in enumerate(grads):
        placed = jnp.where(lane_f == tilt + float(at * TILTS), grad, placed)
    sums_by_series = jnp.zeros((n_se, LANES), F32)
    series_row = lax.broadcasted_iota(jnp.int32, (n_se, LANES), 0)
    for n in range(ITEMS):
        sums_by_series += jnp.where(series_row == series_id[n], placed[n : n + 1, :], 0.0)
    for s in range(n_se):
        series_out[s] = sums_by_series[s : s + 1, :]

    def send_series(k):
        other = (se + k) % n_se
        return remote(series_out.at[other], series_in.at[se], series_send.at[k], series_recv.at[k], (sp, other))

    def take_series(k):
        other = (se + n_se - k) % n_se
        return remote(series_out.at[se], series_in.at[other], series_send.at[k], series_recv.at[k], (sp, other))

    @pl.loop(1, n_se)
    def _(k):
        send_series(k).start()

    series_in[se] = series_out[se]

    @pl.loop(1, n_se)
    def _(k):
        take_series(k).wait_recv()

    species_out[...] = sum(series_in[s] for s in range(n_se))

    def send_species(k):
        other = (sp + k) % n_sp
        return remote(species_out, species_in.at[sp], species_send.at[k], species_recv.at[k], (other, se))

    def take_species(k):
        other = (sp + n_sp - k) % n_sp
        return remote(species_out, species_in.at[other], species_send.at[k], species_recv.at[k], (other, se))

    @pl.loop(1, n_sp)
    def _(k):
        send_species(k).start()

    species_in[sp] = species_out[...]

    @pl.loop(1, n_sp)
    def _(k):
        take_species(k).wait_recv()

    tilts = sum(species_in[s] for s in range(n_sp))
    for at in range(3):
        tilt_out[at] = tilts[:, at * TILTS : (at + 1) * TILTS]

    for k in range(1, NY):
        send_ext(k).wait_send()

    @pl.loop(0, GROUPS)
    def _(g):
        for k in range(1, NY):
            send_item(k, g).wait_send()
        send_tile(0, 0, g, own_tiles, sibling).wait_send()
        send_tile(3, 2, g, own_far, sibling).wait_send()

        @pl.when(g % 2 == x % 2)
        def _():
            send_tile(1, 1, g, own_tiles, mirror).wait_send()
            send_tile(2, 1, g, own_far, beside).wait_send()

    for k in range(1, NY):
        send_part(k).wait_send()

    @pl.loop(1, n_se)
    def _(k):
        send_series(k).wait_send()

    @pl.loop(1, n_sp)
    def _(k):
        send_species(k).wait_send()


def solution(mesh):
    n_sp, n_se = mesh.shape["species"], mesh.shape["series"]
    placed = (
        P(("species", "series"), None),
        P(("species", "series")),
        P(None, ("species", "series")),
        P(("species", "series"), None),
        P(("species", "series"), None),
        P("species", None),
        P(("species", "series")),
        P(("species", "series")),
    )
    table = phase_tables()
    rows = frequency_rows()
    any_space = pl.BlockSpec(memory_space=pl.ANY)
    vmem = pl.BlockSpec(memory_space=pltpu.VMEM)
    smem = pl.BlockSpec(memory_space=pltpu.SMEM)
    dma = pltpu.SemaphoreType.DMA

    def body(observed, defocus, shift_center, pose_index, pose_logprior, reference_tiles, series_id, tilt_id):
        return pl.pallas_call(
            kernel,
            out_shape=(jax.ShapeDtypeStruct((ITEMS,), F32), jax.ShapeDtypeStruct((3, 1, TILTS), F32)),
            in_specs=[any_space, any_space, any_space, vmem, vmem, vmem, smem, smem, smem, smem],
            out_specs=(vmem, vmem),
            scratch_shapes=[
                pltpu.VMEM((ITEMS, 2 * FREQ), BF16),
                pltpu.VMEM((GROUPS, 4, 2, 2 * POSES_SP, WIDTH), BF16),
                pltpu.VMEM((GROUPS, NY, 2, ITEMS, WIDTH), BF16),
                pltpu.VMEM((GROUPS, 2, WIDTH, 3 * LANES), BF16),
                pltpu.VMEM((NY, 2 * ITEMS, LANES), F32),
                pltpu.VMEM((NY, ITEMS, LANES), F32),
                pltpu.VMEM((2, NY, PAIRS * ITEMS, 4 * POSES_SP), BF16),
                pltpu.VMEM((2, NY, ITEMS, FREQ), BF16),
                pltpu.VMEM((4, ROWS, WIDTH), BF16),
                pltpu.VMEM((2, 2, ROWS, 2 * LANES), F32),
                pltpu.VMEM((2, 2, ROWS, LANES), F32),
                pltpu.VMEM((NY, ITEMS, LANES), F32),
                pltpu.VMEM((NY, ITEMS, LANES), F32),
                pltpu.VMEM((n_se, 1, LANES), F32),
                pltpu.VMEM((n_se, 1, LANES), F32),
                pltpu.VMEM((1, LANES), F32),
                pltpu.VMEM((n_sp, 1, LANES), F32),
                dma((2 * GROUPS + 1,)),
                dma((GROUPS,)),
                dma((NY, GROUPS)),
                dma((NY, GROUPS)),
                dma((4, GROUPS)),
                dma((3, GROUPS)),
                dma((NY,)),
                dma((NY,)),
                dma((NY,)),
                dma((NY,)),
                dma((n_se,)),
                dma((n_se,)),
                dma((n_sp,)),
                dma((n_sp,)),
            ],
            compiler_params=pltpu.CompilerParams(
                collective_id=0, has_side_effects=True, vmem_limit_bytes=60 * 2**20
            ),
        )(
            observed,
            reference_tiles,
            jnp.asarray(table),
            jnp.asarray(rows),
            pose_index,
            pose_logprior,
            defocus,
            shift_center,
            series_id,
            tilt_id,
        )

    return jax.shard_map(
        body,
        mesh=mesh,
        in_specs=placed,
        out_specs=(P(("species", "series")), P(None, "series", None)),
        check_vma=False,
    )
```

```python
import functools
import math

import jax
import jax.numpy as jnp
import ml_dtypes
import numpy as np
from jax import lax
from jax.experimental import pallas as pl
from jax.experimental.pallas import tpu as pltpu
from jax.sharding import PartitionSpec as P

MESH = pl.DeviceIdType.MESH
F32 = jnp.float32
BF16 = jnp.bfloat16

BOX = 96
FREQ = 4608
SHIFT_Y = 8
SHIFT_X = 16
POSES_SP = 16
TILTS = 40
SCORE_SCALE = 0.03125
CTF_RATE = 4.0
AMP_PHASE = 0.1
ENV_RATE = 0.5
TWO_PI = 6.283185307179586

GROUPS = 6
WIDTH = FREQ // GROUPS
BLOCKS = GROUPS // 2
DEPTH = 2 * WIDTH
SUB = 256
LANES = 128
ITEMS = 16
NY = 4
NX = 4
NZ = 8
PAIRS = 8
ROWS = NY * PAIRS * ITEMS


def shift_halves():
    window = [(i - SHIFT_Y // 2, j - SHIFT_X // 2) for i in range(SHIFT_Y) for j in range(SHIFT_X)]
    inside = set(window)
    both = [s for s in window if s > (0, 0) and (-s[0], -s[1]) in inside]
    alone = [(0, 0)] + [s for s in window if (-s[0], -s[1]) not in inside]
    return both, alone


BOTH, ALONE = shift_halves()
N_BOTH, N_HALF = len(BOTH), len(BOTH) + len(ALONE)


def sine_fit():
    turn = np.cos(np.pi * (np.arange(400) + 0.5) / 400) * 0.5
    square = turn * turn
    odd = np.stack([turn * square**k for k in range(6)], 1)
    even = np.stack([square**k for k in range(7)], 1)
    sine = np.linalg.lstsq(odd, np.sin(2 * np.pi * turn), rcond=None)[0]
    cosine = np.linalg.lstsq(even, np.cos(2 * np.pi * turn), rcond=None)[0]
    return [float(np.float32(c)) for c in sine], [float(np.float32(c)) for c in cosine]


SINE, COSINE = sine_fit()


def sin_cos(turns):
    turn = turns - jnp.floor(turns + 0.5)
    square = turn * turn
    sine = SINE[-1]
    for c in SINE[-2::-1]:
        sine = sine * square + c
    cosine = COSINE[-1]
    for c in COSINE[-2::-1]:
        cosine = cosine * square + c
    return sine * turn, cosine


def frequencies():
    flat = np.arange(FREQ)
    row, col = flat // (BOX // 2), flat % (BOX // 2)
    return np.where(row < BOX // 2, row, row - BOX).astype(np.float64), col.astype(np.float64)


def frequency_rows():
    freq_y, freq_x = frequencies()
    k2 = (freq_y**2 + freq_x**2) / (BOX / 2.0) ** 2
    env = np.exp(-ENV_RATE * k2)
    rows = np.zeros((8, FREQ), np.float64)
    rows[0] = freq_y
    rows[1] = freq_x
    rows[2] = CTF_RATE * k2 / TWO_PI
    rows[3] = -env
    rows[4] = -CTF_RATE * k2 * env
    return rows.astype(np.float32)


def phase_tables():
    freq_y, freq_x = frequencies()
    half = np.array(BOTH + ALONE, np.float64)
    angle = TWO_PI / BOX * (freq_y[:, None] * half[None, :, 0] + freq_x[:, None] * half[None, :, 1])
    cosine, sine = np.cos(angle), np.sin(angle)
    rate_x, rate_y = (TWO_PI / BOX * freq_x)[:, None], (TWO_PI / BOX * freq_y)[:, None]
    table = np.zeros((2, FREQ, 2 * LANES), np.float64)
    slopes = np.zeros((2, FREQ, LANES), np.float64)
    for part, (value, slope) in enumerate(((cosine, -sine), (sine, cosine))):
        table[part, :, :N_HALF] = value
        table[part, :, N_HALF : N_HALF + N_BOTH] = rate_x * slope[:, :N_BOTH]
        table[part, :, LANES : LANES + N_HALF] = rate_y * slope
        table[part, :, LANES + N_HALF : LANES + 2 * N_HALF - N_BOTH] = rate_x * slope[:, N_BOTH:]
        slopes[part, :, :N_HALF] = value
        slopes[part, :, N_HALF:] = (1 - 2 * part) * value[:, :N_BOTH]
    table = table.reshape(2, BLOCKS, DEPTH, 2 * LANES).transpose(1, 0, 2, 3)
    slopes = slopes.reshape(2, BLOCKS, DEPTH, LANES).transpose(1, 0, 2, 3).reshape(BLOCKS, 2 * DEPTH, LANES)
    return [t.astype(np.float32).astype(ml_dtypes.bfloat16) for t in (table, slopes)]


def kernel(
    observed,
    reference_tiles,
    table_in,
    slopes_in,
    freq_rows,
    pose_index,
    pose_logprior,
    defocus,
    shift_center,
    series_id,
    tilt_id,
    result,
    raw,
    tiles,
    items,
    table,
    slopes,
    ext,
    priors,
    pose_hot,
    ctf,
    lhs,
    lhs_slope,
    acc,
    acc_slope,
    part_out,
    part_in,
    own_loglik,
    xc_out,
    xc_in,
    z_out,
    z_in,
    local_sem,
    table_sem,
    item_send,
    item_recv,
    tile_send,
    tile_recv,
    ext_send,
    ext_recv,
    part_send,
    part_recv,
    xc_send,
    xc_recv,
    z_send,
    z_recv,
):
    sp = lax.axis_index("species")
    se = lax.axis_index("series")
    z_hi, y, core = sp // 8, (sp // 2) % NY, sp % 2
    z_lo, x = se // NX, se % NX
    z, xc = z_hi * 4 + z_lo, x * 2 + core

    def at_y(other):
        return (z_hi * 8 + other * 2 + core, se)

    def at_z(other):
        return (other // 4 * 8 + y * 2 + core, other % 4 * NX + x)

    def at_xc(other):
        return (z_hi * 8 + y * 2 + other % 2, z_lo * NX + other // 2)

    sibling = (z_hi * 8 + y * 2 + 1 - core, se)
    mirror = at_z(NZ - 1 - z)
    beside = (sp, z_lo * NX + x + 1 - 2 * (x % 2))
    own_tiles = z_hi * 2 + core
    own_far = (1 - z_hi) * 2 + core
    sibling_tiles = z_hi * 2 + 1 - core
    sibling_far = (1 - z_hi) * 2 + 1 - core

    barrier = pltpu.get_barrier_semaphore()
    partners = [at_y((y + k) % NY) for k in range(1, NY)]
    partners += [at_xc((xc + k) % (2 * NX)) for k in range(1, 2 * NX)]
    partners += [at_z((z + k) % NZ) for k in range(1, NZ)]
    for partner in partners:
        pl.semaphore_signal(barrier, inc=1, device_id=partner, device_id_type=MESH)

    raw_copy = pltpu.make_async_copy(observed, raw, local_sem.at[2 * GROUPS])
    raw_copy.start()

    def tile_copy(g, part):
        return pltpu.make_async_copy(
            reference_tiles.at[:, pl.ds(pl.multiple_of(part * FREQ + g * WIDTH, WIDTH), WIDTH)],
            tiles.at[g, own_tiles, part],
            local_sem.at[2 * g + part],
        )

    def table_copy(k):
        return pltpu.make_async_copy(table_in.at[k], table.at[k], table_sem.at[k])

    def slopes_copy(k):
        return pltpu.make_async_copy(slopes_in.at[k], slopes.at[k], table_sem.at[BLOCKS + k])

    @pl.loop(0, GROUPS)
    def _(g):
        tile_copy(g, 0).start()
        tile_copy(g, 1).start()

    for k in range(BLOCKS):
        table_copy(k).start()
        slopes_copy(k).start()

    def remote(src, dst, send, recv, device):
        return pltpu.make_async_remote_copy(
            src_ref=src, dst_ref=dst, send_sem=send, recv_sem=recv, device_id=device, device_id_type=MESH
        )

    def send_item(k, g):
        ref = items.at[g, y]
        return remote(ref, ref, item_send.at[k, g], item_recv.at[k, g], at_y((y + k) % NY))

    def take_item(k, g):
        other = (y + NY - k) % NY
        ref = items.at[g, other]
        return remote(ref, ref, item_send.at[k, g], item_recv.at[k, g], at_y(other))

    def send_tile(kind, lane, g, slot, device):
        ref = tiles.at[g, slot]
        return remote(ref, ref, tile_send.at[kind, g], tile_recv.at[lane, g], device)

    def send_ext(k):
        ref = ext.at[y]
        return remote(ref, ref, ext_send.at[k], ext_recv.at[k], at_y((y + k) % NY))

    def take_ext(k):
        other = (y + NY - k) % NY
        ref = ext.at[other]
        return remote(ref, ref, ext_send.at[k], ext_recv.at[k], at_y(other))

    row16 = lax.broadcasted_iota(jnp.int32, (ITEMS, LANES), 0)
    lane16 = lax.broadcasted_iota(jnp.int32, (ITEMS, LANES), 1)

    def column(read):
        out = jnp.zeros((ITEMS, LANES), F32)
        for n in range(ITEMS):
            out = jnp.where(row16 == n, read(n).astype(F32), out)
        return out

    ext[y, :ITEMS, :] = jnp.concatenate([pose_index[...].astype(F32), pose_logprior[...]], 1)
    facts = jnp.where(lane16 == 0, column(lambda n: defocus[n]), column(lambda n: tilt_id[n]))
    ext[y, ITEMS:, :] = jnp.where(lane16 == 2, column(lambda n: series_id[n]), facts)

    center_y = column(lambda n: shift_center[0, n])
    center_x = column(lambda n: shift_center[1, n])
    center_y = jnp.concatenate([center_y, center_y], 1)
    center_x = jnp.concatenate([center_x, center_x], 1)
    raw_copy.wait()

    @pl.loop(0, GROUPS)
    def _(g):
        for sub in range(WIDTH // SUB):
            at = g * WIDTH + sub * SUB
            re_cols = pl.ds(pl.multiple_of(at, SUB), SUB)
            im_cols = pl.ds(pl.multiple_of(FREQ + at, SUB), SUB)
            turns = freq_rows[0:1, re_cols] * center_y + freq_rows[1:2, re_cols] * center_x
            sine, cosine = sin_cos(turns * (1.0 / BOX))
            re, im = raw[:, re_cols].astype(F32), raw[:, im_cols].astype(F32)
            cols = slice(sub * SUB, (sub + 1) * SUB)
            items[g, y, 0, :, cols] = (re * cosine + im * sine).astype(BF16)
            items[g, y, 1, :, cols] = (im * cosine - re * sine).astype(BF16)

    pl.semaphore_wait(barrier, len(partners))

    for k in range(1, NY):
        send_ext(k).start()

    @pl.loop(0, GROUPS)
    def _(g):
        for k in range(1, NY):
            send_item(k, g).start()
        tile_copy(g, 0).wait()
        tile_copy(g, 1).wait()

        @pl.when(g % 2 == x % 2)
        def _():
            send_tile(1, 1, g, own_tiles, mirror).start()

        send_tile(0, 0, g, own_tiles, sibling).start()

    acc[...] = jnp.zeros_like(acc)
    acc_slope[...] = jnp.zeros_like(acc_slope)

    for k in range(1, NY):
        take_ext(k).wait_recv()

    lane_f = lane16.astype(F32)
    to_front = (LANES - 8 * y) % LANES

    @pl.loop(0, NY)
    def _(b):
        moved = pltpu.roll(ext[b, :ITEMS, :], to_front, 1)
        priors[b] = moved
        for h in range(2):
            for j in range(PAIRS):
                pose = moved[:, 32 * h + j : 32 * h + j + 1] + float((j // 2) * POSES_SP)
                hot = jnp.where(lane_f == pose, 1.0, 0.0)[:, : 4 * POSES_SP]
                pose_hot[h, b, j * ITEMS : (j + 1) * ITEMS, :] = hot.astype(BF16)

    @pl.loop(0, NY)
    def _(b):
        focus = ext[b, ITEMS:, 0:1] + jnp.zeros((ITEMS, SUB), F32)

        @pl.loop(0, FREQ // SUB)
        def _(c):
            cols = pl.ds(pl.multiple_of(c * SUB, SUB), SUB)
            turns = focus * freq_rows[2:3, cols] - AMP_PHASE / TWO_PI
            sine, cosine = sin_cos(turns)
            ctf[0, b, :, cols] = (sine * freq_rows[3:4, cols]).astype(BF16)
            ctf[1, b, :, cols] = (cosine * freq_rows[4:5, cols]).astype(BF16)

    def pass_own(g):
        send_tile(1, 1, g, own_far, mirror).wait_recv()
        send_tile(2, 1, g, own_far, beside).start()
        send_tile(3, 2, g, own_far, sibling).start()

    def pass_other(g):
        send_tile(2, 1, g, own_far, beside).wait_recv()
        send_tile(3, 2, g, own_far, sibling).start()

    def fill(g, h, part):
        for sub in range(WIDTH // SUB):
            cols = slice(sub * SUB, (sub + 1) * SUB)
            tile_re = tiles[g, pl.ds(2 * h, 2), 0, :, cols].reshape(4 * POSES_SP, SUB)
            tile_im = tiles[g, pl.ds(2 * h, 2), 1, :, cols].reshape(4 * POSES_SP, SUB)
            freqs = pl.ds(pl.multiple_of(g * WIDTH + sub * SUB, SUB), SUB)
            at = part * WIDTH + sub * SUB
            for b in range(NY):
                hot = pose_hot[h, b]
                re = jnp.dot(hot, tile_re, preferred_element_type=F32).reshape(PAIRS, ITEMS, SUB).astype(BF16)
                im = jnp.dot(hot, tile_im, preferred_element_type=F32).reshape(PAIRS, ITEMS, SUB).astype(BF16)
                value, slope = ctf[0, b, :, freqs], ctf[1, b, :, freqs]
                o_re, o_im = items[g, b, 0, :, cols], items[g, b, 1, :, cols]
                prod_re = re * o_re + im * o_im
                prod_im = re * o_im - im * o_re
                rows = slice(b * PAIRS * ITEMS, (b + 1) * PAIRS * ITEMS)
                lhs[0, rows, at : at + SUB] = (prod_re * value).reshape(PAIRS * ITEMS, SUB)
                lhs[1, rows, at : at + SUB] = (prod_im * value).reshape(PAIRS * ITEMS, SUB)
                lhs_slope[rows, at : at + SUB] = (prod_re * slope).reshape(PAIRS * ITEMS, SUB)
                lhs_slope[rows, DEPTH + at : DEPTH + at + SUB] = (prod_im * slope).reshape(PAIRS * ITEMS, SUB)

    passing = ((0, 0, 0, True), (1, 0, 1, True), (1, 1, 0, False), (2, 0, 1, False), (2, 1, 2, True), (4, 0, 2, False))

    @pl.loop(0, 2 * BLOCKS)
    def _(i):
        far = jnp.where(i < 2, 0, jnp.where(i == 3, 0, 1))
        block = jnp.where(i < 2, i, jnp.where(i == 2, 0, jnp.where(i == 3, 2, i - 3)))
        h = (z_hi + far) % 2
        for part in range(2):
            g = 2 * block + part

            @pl.when(far == 0)
            def _(g=g):
                for k in range(1, NY):
                    take_item(k, g).wait_recv()
                send_tile(0, 0, g, sibling_tiles, sibling).wait_recv()

            @pl.when(far == 1)
            def _(g=g):
                send_tile(3, 2, g, sibling_far, sibling).wait_recv()

            fill(g, h, part)
            for at, at_part, k, own in passing:
                if at_part == part:

                    @pl.when(i == at)
                    def _(k=k, own=own):
                        if own:
                            pass_own(2 * k + x % 2)
                        else:
                            pass_other(2 * k + 1 - x % 2)

        @pl.when(far == 0)
        def _():
            table_copy(block).wait()
            slopes_copy(block).wait()

        for q in range(2):
            acc[h, q] += jnp.dot(lhs[q], table[block, q], preferred_element_type=F32)
        acc_slope[h] += jnp.dot(lhs_slope[...], slopes[block], preferred_element_type=F32)

    plus_ok, minus_ok = lane16 < N_HALF, lane16 < N_BOTH
    lowest = -1e30

    @pl.loop(0, NY)
    def _(b):
        message = priors[b]
        places = []
        for h in range(2):
            for j in range(PAIRS):
                places.append((h, j, pl.ds(pl.multiple_of((b * PAIRS + j) * ITEMS, ITEMS), ITEMS)))
        scores = []
        for h, j, rows in places:
            prior = message[:, 64 + 32 * h + j : 64 + 32 * h + j + 1]
            re, im = acc[h, 0, rows, :LANES], acc[h, 1, rows, :LANES]
            scores.append(
                (
                    jnp.where(plus_ok, SCORE_SCALE * (re + im) + prior, lowest),
                    jnp.where(minus_ok, SCORE_SCALE * (re - im) + prior, lowest),
                )
            )
        top = functools.reduce(jnp.maximum, [jnp.maximum(p, m) for p, m in scores])
        top = jnp.max(top, axis=1, keepdims=True)
        zero = jnp.zeros((ITEMS, LANES), F32)
        total, d_focus, d_x, d_x_alone, d_y = zero, zero, zero, zero, zero
        for (h, j, rows), (p, m) in zip(places, scores):
            p, m = jnp.exp(p - top), jnp.exp(m - top)
            total += p + m
            m_moved = pltpu.roll(m, N_HALF, 1)
            d_focus += (p + m_moved) * acc_slope[h, rows, :]
            re, im = acc[h, 0, rows, :LANES], acc[h, 1, rows, :LANES]
            d_x += pltpu.roll(p, N_HALF, 1) * (re + im) - m_moved * (re - im)
            re, im = acc[h, 0, rows, LANES:], acc[h, 1, rows, LANES:]
            d_y += p * (re + im) - m * (re - im)
            d_x_alone += pltpu.roll(p, N_HALF - N_BOTH, 1) * (re + im)
        d_x = jnp.where(lane16 >= N_HALF, d_x, 0.0)
        d_x += jnp.where((lane16 >= N_HALF) & (lane16 < 2 * N_HALF - N_BOTH), d_x_alone, 0.0)
        out = jnp.where(lane16 == 0, top, 0.0)
        for at, term in enumerate((total, d_focus, d_x, d_y)):
            out = jnp.where(lane16 == at + 1, jnp.sum(term, axis=1, keepdims=True), out)
        part_out[b] = out

    def send_part(k):
        other = (y + k) % NY
        return remote(part_out, part_in.at[y], part_send.at[k], part_recv.at[k], at_y(other))

    def take_part(k):
        other = (y + NY - k) % NY
        return remote(part_out, part_in.at[other], part_send.at[k], part_recv.at[k], at_y(other))

    for k in range(1, NY):
        send_part(k).start()
    part_in[y] = part_out[...]

    tilt, series = [], []
    for b in range(NY):
        tilt.append(ext[b, ITEMS:, 1:2] + jnp.zeros((ITEMS, LANES), F32))
        series.append(ext[b, ITEMS:, 2:3] + jnp.zeros((ITEMS, LANES), F32))
    for k in range(1, NY):
        take_part(k).wait_recv()

    placed = []
    for b in range(NY):
        parts = [part_in[src, b] for src in range(NY)]
        tops = [part[:, 0:1] for part in parts]
        top = functools.reduce(jnp.maximum, tops)
        sums = sum(part * jnp.exp(t - top) for part, t in zip(parts, tops))
        grads = sums * SCORE_SCALE / sums[:, 1:2]
        spread = jnp.zeros((ITEMS, LANES), F32)
        for at in range(3):
            spread = jnp.where(lane_f == tilt[b] + float(at * TILTS), grads[:, 2 + at : 3 + at], spread)
        placed.append(spread)
        own_loglik[b] = top + jnp.log(sums[:, 1:2]) + jnp.zeros((ITEMS, LANES), F32)
    row8 = lax.broadcasted_iota(jnp.int32, (8, LANES), 0)
    for to in range(NX):
        rows = jnp.zeros((8, LANES), F32)
        for lo in range(4):
            hits = [jnp.where(s == float(lo * NX + to), p, 0.0) for s, p in zip(series, placed)]
            rows = jnp.where(row8 == lo, jnp.sum(sum(hits), axis=0, keepdims=True), rows)
        xc_out[to] = rows

    def send_xc(k):
        other = (xc + k) % (2 * NX)
        return remote(xc_out.at[other // 2], xc_in.at[xc], xc_send.at[k], xc_recv.at[k], at_xc(other))

    def take_xc(k):
        other = (xc + 2 * NX - k) % (2 * NX)
        return remote(xc_out.at[x], xc_in.at[other], xc_send.at[k], xc_recv.at[k], at_xc(other))

    for k in range(1, 2 * NX):
        send_xc(k).start()
    xc_in[xc] = xc_out[x]
    loglik = own_loglik[y]
    result[0:1, :] = jnp.sum(jnp.where(row16 == lane16, loglik, 0.0), axis=0, keepdims=True)
    for k in range(1, 2 * NX):
        take_xc(k).wait_recv()
    rows = sum(xc_in[k] for k in range(2 * NX))
    for lo in range(4):
        z_out[lo] = rows[lo : lo + 1]

    def send_z(k):
        other = (z + k) % NZ
        return remote(z_out.at[other % 4], z_in.at[z], z_send.at[k], z_recv.at[k], at_z(other))

    def take_z(k):
        other = (z + NZ - k) % NZ
        return remote(z_out.at[z_lo], z_in.at[other], z_send.at[k], z_recv.at[k], at_z(other))

    for k in range(1, NZ):
        send_z(k).start()
    z_in[z] = z_out[z_lo]
    for k in range(1, NZ):
        take_z(k).wait_recv()
    result[1:2, :] = sum(z_in[k] for k in range(NZ))

    for k in range(1, NY):
        send_ext(k).wait_send()

    @pl.loop(0, GROUPS)
    def _(g):
        for k in range(1, NY):
            send_item(k, g).wait_send()
        send_tile(0, 0, g, own_tiles, sibling).wait_send()
        send_tile(3, 2, g, own_far, sibling).wait_send()

        @pl.when(g % 2 == x % 2)
        def _():
            send_tile(1, 1, g, own_tiles, mirror).wait_send()
            send_tile(2, 1, g, own_far, beside).wait_send()

    for k in range(1, NY):
        send_part(k).wait_send()

    for k in range(1, 2 * NX):
        send_xc(k).wait_send()
    for k in range(1, NZ):
        send_z(k).wait_send()


def finish(result, loglik_out, tilt_out):
    loglik_out[...] = result[0, :ITEMS]
    for at in range(3):
        tilt_out[at] = result[1:2, at * TILTS : (at + 1) * TILTS]


def solution(mesh):
    placed = (
        P(("species", "series"), None),
        P(("species", "series")),
        P(None, ("species", "series")),
        P(("species", "series"), None),
        P(("species", "series"), None),
        P("species", None),
        P(("species", "series")),
        P(("species", "series")),
    )
    table, slopes = phase_tables()
    rows = frequency_rows()
    any_space = pl.BlockSpec(memory_space=pl.ANY)
    vmem = pl.BlockSpec(memory_space=pltpu.VMEM)
    smem = pl.BlockSpec(memory_space=pltpu.SMEM)
    dma = pltpu.SemaphoreType.DMA

    def body(observed, defocus, shift_center, pose_index, pose_logprior, reference_tiles, series_id, tilt_id):
        result = pl.pallas_call(
            kernel,
            out_shape=jax.ShapeDtypeStruct((8, LANES), F32),
            in_specs=[any_space, any_space, any_space, any_space, vmem, vmem, vmem, smem, smem, smem, smem],
            out_specs=vmem,
            scratch_shapes=[
                pltpu.VMEM((ITEMS, 2 * FREQ), BF16),
                pltpu.VMEM((GROUPS, 4, 2, 2 * POSES_SP, WIDTH), BF16),
                pltpu.VMEM((GROUPS, NY, 2, ITEMS, WIDTH), BF16),
                pltpu.VMEM((BLOCKS, 2, DEPTH, 2 * LANES), BF16),
                pltpu.VMEM((BLOCKS, 2 * DEPTH, LANES), BF16),
                pltpu.VMEM((NY, 2 * ITEMS, LANES), F32),
                pltpu.VMEM((NY, ITEMS, LANES), F32),
                pltpu.VMEM((2, NY, PAIRS * ITEMS, 4 * POSES_SP), BF16),
                pltpu.VMEM((2, NY, ITEMS, FREQ), BF16),
                pltpu.VMEM((2, ROWS, DEPTH), BF16),
                pltpu.VMEM((ROWS, 2 * DEPTH), BF16),
                pltpu.VMEM((2, 2, ROWS, 2 * LANES), F32),
                pltpu.VMEM((2, ROWS, LANES), F32),
                pltpu.VMEM((NY, ITEMS, LANES), F32),
                pltpu.VMEM((NY, NY, ITEMS, LANES), F32),
                pltpu.VMEM((NY, ITEMS, LANES), F32),
                pltpu.VMEM((NX, 8, LANES), F32),
                pltpu.VMEM((2 * NX, 8, LANES), F32),
                pltpu.VMEM((4, 1, LANES), F32),
                pltpu.VMEM((NZ, 1, LANES), F32),
                dma((2 * GROUPS + 1,)),
                dma((2 * BLOCKS,)),
                dma((NY, GROUPS)),
                dma((NY, GROUPS)),
                dma((4, GROUPS)),
                dma((3, GROUPS)),
                dma((NY,)),
                dma((NY,)),
                dma((NY,)),
                dma((NY,)),
                dma((2 * NX,)),
                dma((2 * NX,)),
                dma((NZ,)),
                dma((NZ,)),
            ],
            compiler_params=pltpu.CompilerParams(
                collective_id=0, has_side_effects=True, vmem_limit_bytes=60 * 2**20
            ),
        )(
            observed,
            reference_tiles,
            jnp.asarray(table),
            jnp.asarray(slopes),
            jnp.asarray(rows),
            pose_index,
            pose_logprior,
            defocus,
            shift_center,
            series_id,
            tilt_id,
        )
        return pl.pallas_call(
            finish,
            out_shape=(jax.ShapeDtypeStruct((ITEMS,), F32), jax.ShapeDtypeStruct((3, 1, TILTS), F32)),
            in_specs=[vmem],
            out_specs=(vmem, vmem),
        )(result)

    return jax.shard_map(
        body,
        mesh=mesh,
        in_specs=placed,
        out_specs=(P(("species", "series")), P(None, "series", None)),
        check_vma=False,
    )
```

```python
import functools
import math

import jax
import jax.numpy as jnp
import ml_dtypes
import numpy as np
from jax import lax
from jax.experimental import pallas as pl
from jax.experimental.pallas import tpu as pltpu
from jax.sharding import PartitionSpec as P

MESH = pl.DeviceIdType.MESH
F32 = jnp.float32
BF16 = jnp.bfloat16

BOX = 96
FREQ = 4608
SHIFT_Y = 8
SHIFT_X = 16
POSES_SP = 16
TILTS = 40
SCORE_SCALE = 0.03125
CTF_RATE = 4.0
AMP_PHASE = 0.1
ENV_RATE = 0.5
TWO_PI = 6.283185307179586

GROUPS = 6
WIDTH = FREQ // GROUPS
BLOCKS = GROUPS // 2
DEPTH = 2 * WIDTH
SUB = 256
LANES = 128
ITEMS = 16
NY = 4
NX = 4
NZ = 8
UNIT = WIDTH // 2
PAIRS = 8
ROWS = NY * PAIRS * ITEMS


def shift_halves():
    window = [(i - SHIFT_Y // 2, j - SHIFT_X // 2) for i in range(SHIFT_Y) for j in range(SHIFT_X)]
    inside = set(window)
    both = [s for s in window if s > (0, 0) and (-s[0], -s[1]) in inside]
    alone = [(0, 0)] + [s for s in window if (-s[0], -s[1]) not in inside]
    return both, alone


BOTH, ALONE = shift_halves()
N_BOTH, N_HALF = len(BOTH), len(BOTH) + len(ALONE)


def sine_fit():
    turn = np.cos(np.pi * (np.arange(400) + 0.5) / 400) * 0.5
    square = turn * turn
    odd = np.stack([turn * square**k for k in range(6)], 1)
    even = np.stack([square**k for k in range(7)], 1)
    sine = np.linalg.lstsq(odd, np.sin(2 * np.pi * turn), rcond=None)[0]
    cosine = np.linalg.lstsq(even, np.cos(2 * np.pi * turn), rcond=None)[0]
    return [float(np.float32(c)) for c in sine], [float(np.float32(c)) for c in cosine]


SINE, COSINE = sine_fit()


def sin_cos(turns):
    turn = turns - jnp.floor(turns + 0.5)
    square = turn * turn
    sine = SINE[-1]
    for c in SINE[-2::-1]:
        sine = sine * square + c
    cosine = COSINE[-1]
    for c in COSINE[-2::-1]:
        cosine = cosine * square + c
    return sine * turn, cosine


def frequencies():
    flat = np.arange(FREQ)
    row, col = flat // (BOX // 2), flat % (BOX // 2)
    return np.where(row < BOX // 2, row, row - BOX).astype(np.float64), col.astype(np.float64)


def frequency_rows():
    freq_y, freq_x = frequencies()
    k2 = (freq_y**2 + freq_x**2) / (BOX / 2.0) ** 2
    env = np.exp(-ENV_RATE * k2)
    rows = np.zeros((8, FREQ), np.float64)
    rows[0] = freq_y
    rows[1] = freq_x
    rows[2] = CTF_RATE * k2 / TWO_PI
    rows[3] = -env
    rows[4] = -CTF_RATE * k2 * env
    return rows.astype(np.float32)


def phase_tables():
    freq_y, freq_x = frequencies()
    half = np.array(BOTH + ALONE, np.float64)
    angle = TWO_PI / BOX * (freq_y[:, None] * half[None, :, 0] + freq_x[:, None] * half[None, :, 1])
    cosine, sine = np.cos(angle), np.sin(angle)
    rate_x, rate_y = (TWO_PI / BOX * freq_x)[:, None], (TWO_PI / BOX * freq_y)[:, None]
    table = np.zeros((2, FREQ, 2 * LANES), np.float64)
    slopes = np.zeros((2, FREQ, LANES), np.float64)
    for part, (value, slope) in enumerate(((cosine, -sine), (sine, cosine))):
        table[part, :, :N_HALF] = value
        table[part, :, N_HALF : N_HALF + N_BOTH] = rate_x * slope[:, :N_BOTH]
        table[part, :, LANES : LANES + N_HALF] = rate_y * slope
        table[part, :, LANES + N_HALF : LANES + 2 * N_HALF - N_BOTH] = rate_x * slope[:, N_BOTH:]
        slopes[part, :, :N_HALF] = value
        slopes[part, :, N_HALF:] = (1 - 2 * part) * value[:, :N_BOTH]
    table = table.reshape(2, BLOCKS, DEPTH, 2 * LANES).transpose(1, 0, 2, 3)
    slopes = slopes.reshape(2, BLOCKS, DEPTH, LANES).transpose(1, 0, 2, 3).reshape(BLOCKS, 2 * DEPTH, LANES)
    return [t.astype(np.float32).astype(ml_dtypes.bfloat16) for t in (table, slopes)]


def kernel(
    observed,
    reference_tiles,
    table_in,
    slopes_in,
    freq_rows,
    pose_index,
    pose_logprior,
    defocus,
    shift_center,
    series_id,
    tilt_id,
    result,
    raw,
    tiles,
    items,
    table,
    slopes,
    ext,
    priors,
    pose_hot,
    ctf,
    lhs,
    lhs_slope,
    acc,
    acc_slope,
    part_out,
    part_in,
    own_loglik,
    xc_out,
    xc_in,
    z_out,
    z_in,
    local_sem,
    table_sem,
    item_send,
    item_recv,
    near_send,
    near_recv,
    far_send,
    far_recv,
    sib_send,
    sib_recv,
    ext_send,
    ext_recv,
    part_send,
    part_recv,
    xc_send,
    xc_recv,
    z_send,
    z_recv,
):
    sp = lax.axis_index("species")
    se = lax.axis_index("series")
    z_hi, y, core = sp // 8, (sp // 2) % NY, sp % 2
    z_lo, x = se // NX, se % NX
    z, xc = z_hi * 4 + z_lo, x * 2 + core

    def at_y(other):
        return (z_hi * 8 + other * 2 + core, se)

    def at_z(other):
        return (other // 4 * 8 + y * 2 + core, other % 4 * NX + x)

    def at_xc(other):
        return (z_hi * 8 + y * 2 + other % 2, z_lo * NX + other // 2)

    sibling = (z_hi * 8 + y * 2 + 1 - core, se)
    mirror = at_z(NZ - 1 - z)
    own_tiles = z_hi * 2 + core
    own_far = (1 - z_hi) * 2 + core
    sibling_tiles = z_hi * 2 + 1 - core
    sibling_far = (1 - z_hi) * 2 + 1 - core

    barrier = pltpu.get_barrier_semaphore()
    partners = [at_y((y + k) % NY) for k in range(1, NY)]
    partners += [at_xc((xc + k) % (2 * NX)) for k in range(1, 2 * NX)]
    partners += [at_z((z + k) % NZ) for k in range(1, NZ)]
    for partner in partners:
        pl.semaphore_signal(barrier, inc=1, device_id=partner, device_id_type=MESH)

    raw_copy = pltpu.make_async_copy(observed, raw, local_sem.at[2 * GROUPS])
    raw_copy.start()

    def tile_copy(g, part):
        return pltpu.make_async_copy(
            reference_tiles.at[:, pl.ds(pl.multiple_of(part * FREQ + g * WIDTH, WIDTH), WIDTH)],
            tiles.at[g, own_tiles, part],
            local_sem.at[2 * g + part],
        )

    def table_copy(k):
        return pltpu.make_async_copy(table_in.at[k], table.at[k], table_sem.at[k])

    def slopes_copy(k):
        return pltpu.make_async_copy(slopes_in.at[k], slopes.at[k], table_sem.at[BLOCKS + k])

    @pl.loop(0, GROUPS)
    def _(g):
        tile_copy(g, 0).start()
        tile_copy(g, 1).start()

    def remote(src, dst, send, recv, device):
        return pltpu.make_async_remote_copy(
            src_ref=src, dst_ref=dst, send_sem=send, recv_sem=recv, device_id=device, device_id_type=MESH
        )

    def send_item(k, g):
        ref = items.at[g, y]
        return remote(ref, ref, item_send.at[k, g], item_recv.at[k, g], at_y((y + k) % NY))

    def take_item(k, g):
        other = (y + NY - k) % NY
        ref = items.at[g, other]
        return remote(ref, ref, item_send.at[k, g], item_recv.at[k, g], at_y(other))

    def send_near(g):
        ref = tiles.at[g, own_tiles]
        return remote(ref, ref, near_send.at[g], near_recv.at[g], sibling)

    def take_near(g):
        ref = tiles.at[g, sibling_tiles]
        return remote(ref, ref, near_send.at[g], near_recv.at[g], sibling)

    def unit(slot, u):
        return tiles.at[u // 2, slot, :, :, pl.ds(pl.multiple_of(u % 2 * UNIT, UNIT), UNIT)]

    def send_mirror(k):
        ref, u = unit(own_tiles, NX * k + x), NX * k + x
        return remote(ref, ref, far_send.at[0, k], far_recv.at[u], mirror)

    def send_x(j, k):
        ref, u = unit(own_far, NX * k + x), NX * k + x
        return remote(ref, ref, far_send.at[j, k], far_recv.at[u], (sp, z_lo * NX + (x + j) % NX))

    def take_far(j, k):
        u = NX * k + (x + j) % NX
        ref = unit(own_far, u)
        return remote(ref, ref, far_send.at[j, k], far_recv.at[u], mirror)

    def send_sibling(u):
        ref = unit(own_far, u)
        return remote(ref, ref, sib_send.at[u], sib_recv.at[u], sibling)

    def take_sibling(u):
        ref = unit(sibling_far, u)
        return remote(ref, ref, sib_send.at[u], sib_recv.at[u], sibling)

    def send_ext(k):
        ref = ext.at[y]
        return remote(ref, ref, ext_send.at[k], ext_recv.at[k], at_y((y + k) % NY))

    def take_ext(k):
        other = (y + NY - k) % NY
        ref = ext.at[other]
        return remote(ref, ref, ext_send.at[k], ext_recv.at[k], at_y(other))

    row16 = lax.broadcasted_iota(jnp.int32, (ITEMS, LANES), 0)
    lane16 = lax.broadcasted_iota(jnp.int32, (ITEMS, LANES), 1)

    def column(read):
        out = jnp.zeros((ITEMS, LANES), F32)
        for n in range(ITEMS):
            out = jnp.where(row16 == n, read(n).astype(F32), out)
        return out

    ext[y, :ITEMS, :] = jnp.concatenate([pose_index[...].astype(F32), pose_logprior[...]], 1)
    facts = jnp.where(lane16 == 0, column(lambda n: defocus[n]), column(lambda n: tilt_id[n]))
    ext[y, ITEMS:, :] = jnp.where(lane16 == 2, column(lambda n: series_id[n]), facts)

    center_y = column(lambda n: shift_center[0, n])
    center_x = column(lambda n: shift_center[1, n])
    center_y = jnp.concatenate([center_y, center_y], 1)
    center_x = jnp.concatenate([center_x, center_x], 1)
    pl.semaphore_wait(barrier, len(partners))

    for k in (2, 1, 3):
        send_ext(k).start()
    raw_copy.wait()

    @pl.loop(0, GROUPS)
    def _(g):
        for sub in range(WIDTH // SUB):
            at = g * WIDTH + sub * SUB
            re_cols = pl.ds(pl.multiple_of(at, SUB), SUB)
            im_cols = pl.ds(pl.multiple_of(FREQ + at, SUB), SUB)
            turns = freq_rows[0:1, re_cols] * center_y + freq_rows[1:2, re_cols] * center_x
            sine, cosine = sin_cos(turns * (1.0 / BOX))
            re, im = raw[:, re_cols].astype(F32), raw[:, im_cols].astype(F32)
            cols = slice(sub * SUB, (sub + 1) * SUB)
            items[g, y, 0, :, cols] = (re * cosine + im * sine).astype(BF16)
            items[g, y, 1, :, cols] = (im * cosine - re * sine).astype(BF16)
        for k in (2, 1, 3):
            send_item(k, g).start()
        tile_copy(g, 0).wait()
        tile_copy(g, 1).wait()

        for half in range(2):

            @pl.when((2 * g + half) % NX == x)
            def _(half=half):
                send_mirror((2 * g + half) // NX).start()

        send_near(g).start()

    for k in range(BLOCKS):
        table_copy(k).start()
        slopes_copy(k).start()
    acc[...] = jnp.zeros_like(acc)
    acc_slope[...] = jnp.zeros_like(acc_slope)

    lane_f = lane16.astype(F32)
    to_front = (LANES - 8 * y) % LANES

    @pl.loop(0, NY)
    def _(k):
        @pl.when(k > 0)
        def _():
            take_ext(k).wait_recv()

        b = (y + NY - k) % NY
        moved = pltpu.roll(ext[b, :ITEMS, :], to_front, 1)
        priors[b] = moved
        for h in range(2):
            for j in range(PAIRS):
                pose = moved[:, 32 * h + j : 32 * h + j + 1] + float((j // 2) * POSES_SP)
                hot = jnp.where(lane_f == pose, 1.0, 0.0)[:, : 4 * POSES_SP]
                pose_hot[h, b, j * ITEMS : (j + 1) * ITEMS, :] = hot.astype(BF16)
        focus = ext[b, ITEMS:, 0:1] + jnp.zeros((ITEMS, WIDTH), F32)

        @pl.loop(0, GROUPS)
        def _(g):
            cols = pl.ds(pl.multiple_of(g * WIDTH, WIDTH), WIDTH)
            turns = focus * freq_rows[2:3, cols] - AMP_PHASE / TWO_PI
            sine, cosine = sin_cos(turns)
            ctf[0, b, :, cols] = (sine * freq_rows[3:4, cols]).astype(BF16)
            ctf[1, b, :, cols] = (cosine * freq_rows[4:5, cols]).astype(BF16)

    def pass_own(k):
        take_far(0, k).wait_recv()
        for j in (2, 1, 3):
            send_x(j, k).start()
        send_sibling(NX * k + x).start()

    def pass_other(k):
        for j in range(1, NX):
            take_far(j, k).wait_recv()
            send_sibling(NX * k + (x + j) % NX).start()

    def fill(g, h, part):
        for sub in range(WIDTH // SUB):
            cols = slice(sub * SUB, (sub + 1) * SUB)
            tile_re = tiles[g, pl.ds(2 * h, 2), 0, :, cols].reshape(4 * POSES_SP, SUB)
            tile_im = tiles[g, pl.ds(2 * h, 2), 1, :, cols].reshape(4 * POSES_SP, SUB)
            freqs = pl.ds(pl.multiple_of(g * WIDTH + sub * SUB, SUB), SUB)
            at = part * WIDTH + sub * SUB
            for b in range(NY):
                hot = pose_hot[h, b]
                re = jnp.dot(hot, tile_re, preferred_element_type=F32).reshape(PAIRS, ITEMS, SUB).astype(BF16)
                im = jnp.dot(hot, tile_im, preferred_element_type=F32).reshape(PAIRS, ITEMS, SUB).astype(BF16)
                value, slope = ctf[0, b, :, freqs], ctf[1, b, :, freqs]
                o_re, o_im = items[g, b, 0, :, cols], items[g, b, 1, :, cols]
                prod_re = re * o_re + im * o_im
                prod_im = re * o_im - im * o_re
                rows = slice(b * PAIRS * ITEMS, (b + 1) * PAIRS * ITEMS)
                lhs[0, rows, at : at + SUB] = (prod_re * value).reshape(PAIRS * ITEMS, SUB)
                lhs[1, rows, at : at + SUB] = (prod_im * value).reshape(PAIRS * ITEMS, SUB)
                lhs_slope[rows, at : at + SUB] = (prod_re * slope).reshape(PAIRS * ITEMS, SUB)
                lhs_slope[rows, DEPTH + at : DEPTH + at + SUB] = (prod_im * slope).reshape(PAIRS * ITEMS, SUB)

    passing = ((0, 0, 0, True), (0, 1, 1, True), (1, 0, 2, True), (1, 1, 0, False), (2, 0, 1, False), (2, 1, 2, False))

    @pl.loop(0, 2 * BLOCKS)
    def _(i):
        far = jnp.where(i < 2, 0, jnp.where(i == 3, 0, 1))
        block = jnp.where(i < 2, i, jnp.where(i == 2, 0, jnp.where(i == 3, 2, i - 3)))
        h = (z_hi + far) % 2
        for part in range(2):
            g = 2 * block + part

            @pl.when(far == 0)
            def _(g=g):
                for k in range(1, NY):
                    take_item(k, g).wait_recv()
                take_near(g).wait_recv()

            @pl.when(far == 1)
            def _(g=g):
                take_sibling(2 * g).wait_recv()
                take_sibling(2 * g + 1).wait_recv()

            fill(g, h, part)
            for at, at_part, k, own in passing:
                if at_part == part:

                    @pl.when(i == at)
                    def _(k=k, own=own):
                        if own:
                            pass_own(k)
                        else:
                            pass_other(k)

        @pl.when(far == 0)
        def _():
            table_copy(block).wait()
            slopes_copy(block).wait()

        for q in range(2):
            acc[h, q] += jnp.dot(lhs[q], table[block, q], preferred_element_type=F32)
        acc_slope[h] += jnp.dot(lhs_slope[...], slopes[block], preferred_element_type=F32)

    plus_ok, minus_ok = lane16 < N_HALF, lane16 < N_BOTH
    lowest = -1e30
    part_out[...] = jnp.zeros_like(part_out)

    @pl.loop(0, NY)
    def _(b):
        message = priors[b]
        places = []
        for h in range(2):
            for j in range(PAIRS):
                places.append((h, j, pl.ds(pl.multiple_of((b * PAIRS + j) * ITEMS, ITEMS), ITEMS)))
        scores = []
        for h, j, rows in places:
            prior = message[:, 64 + 32 * h + j : 64 + 32 * h + j + 1]
            re, im = acc[h, 0, rows, :LANES], acc[h, 1, rows, :LANES]
            scores.append(
                (
                    jnp.where(plus_ok, SCORE_SCALE * (re + im) + prior, lowest),
                    jnp.where(minus_ok, SCORE_SCALE * (re - im) + prior, lowest),
                )
            )
        top = functools.reduce(jnp.maximum, [jnp.maximum(p, m) for p, m in scores])
        top = jnp.max(top, axis=1, keepdims=True)
        zero = jnp.zeros((ITEMS, LANES), F32)
        total, d_focus, d_x, d_x_alone, d_y = zero, zero, zero, zero, zero
        for (h, j, rows), (p, m) in zip(places, scores):
            p, m = jnp.exp(p - top), jnp.exp(m - top)
            total += p + m
            m_moved = pltpu.roll(m, N_HALF, 1)
            d_focus += (p + m_moved) * acc_slope[h, rows, :]
            re, im = acc[h, 0, rows, :LANES], acc[h, 1, rows, :LANES]
            d_x += pltpu.roll(p, N_HALF, 1) * (re + im) - m_moved * (re - im)
            re, im = acc[h, 0, rows, LANES:], acc[h, 1, rows, LANES:]
            d_y += p * (re + im) - m * (re - im)
            d_x_alone += pltpu.roll(p, N_HALF - N_BOTH, 1) * (re + im)
        d_x = jnp.where(lane16 >= N_HALF, d_x, 0.0)
        d_x += jnp.where((lane16 >= N_HALF) & (lane16 < 2 * N_HALF - N_BOTH), d_x_alone, 0.0)
        out = jnp.where(lane16 == 8 * b, top, part_out[...])
        for at, term in enumerate((total, d_focus, d_x, d_y)):
            out = jnp.where(lane16 == 8 * b + at + 1, jnp.sum(term, axis=1, keepdims=True), out)
        part_out[...] = out

    def send_part(k):
        other = (y + k) % NY
        return remote(part_out, part_in.at[y], part_send.at[k], part_recv.at[k], at_y(other))

    def take_part(k):
        other = (y + NY - k) % NY
        return remote(part_out, part_in.at[other], part_send.at[k], part_recv.at[k], at_y(other))

    for k in range(1, NY):
        send_part(k).start()
    part_in[y] = part_out[...]

    tilt, series = [], []
    for b in range(NY):
        tilt.append(ext[b, ITEMS:, 1:2] + jnp.zeros((ITEMS, LANES), F32))
        series.append(ext[b, ITEMS:, 2:3] + jnp.zeros((ITEMS, LANES), F32))
    for k in range(1, NY):
        take_part(k).wait_recv()

    placed = []
    for b in range(NY):
        parts = [part_in[src] for src in range(NY)]
        at_b = 8 * b
        tops = [part[:, at_b : at_b + 1] for part in parts]
        top = functools.reduce(jnp.maximum, tops)
        sums = sum(part * jnp.exp(t - top) for part, t in zip(parts, tops))
        total = sums[:, at_b + 1 : at_b + 2]
        grads = sums * SCORE_SCALE / total
        spread = jnp.zeros((ITEMS, LANES), F32)
        for at in range(3):
            spread = jnp.where(lane_f == tilt[b] + float(at * TILTS), grads[:, at_b + 2 + at : at_b + 3 + at], spread)
        placed.append(spread)
        own_loglik[b] = top + jnp.log(total) + jnp.zeros((ITEMS, LANES), F32)
    row8 = lax.broadcasted_iota(jnp.int32, (8, LANES), 0)
    for to in range(NX):
        rows = jnp.zeros((8, LANES), F32)
        for lo in range(4):
            hits = [jnp.where(s == float(lo * NX + to), p, 0.0) for s, p in zip(series, placed)]
            rows = jnp.where(row8 == lo, jnp.sum(sum(hits), axis=0, keepdims=True), rows)
        xc_out[to] = rows

    def send_xc(k):
        other = (xc + k) % (2 * NX)
        return remote(xc_out.at[other // 2], xc_in.at[xc], xc_send.at[k], xc_recv.at[k], at_xc(other))

    def take_xc(k):
        other = (xc + 2 * NX - k) % (2 * NX)
        return remote(xc_out.at[x], xc_in.at[other], xc_send.at[k], xc_recv.at[k], at_xc(other))

    for k in range(1, 2 * NX):
        send_xc(k).start()
    xc_in[xc] = xc_out[x]
    loglik = own_loglik[y]
    result[0:1, :] = jnp.sum(jnp.where(row16 == lane16, loglik, 0.0), axis=0, keepdims=True)
    for k in range(1, 2 * NX):
        take_xc(k).wait_recv()
    rows = sum(xc_in[k] for k in range(2 * NX))
    for lo in range(4):
        z_out[lo] = rows[lo : lo + 1]

    def send_z(k):
        other = (z + k) % NZ
        return remote(z_out.at[other % 4], z_in.at[z], z_send.at[k], z_recv.at[k], at_z(other))

    def take_z(k):
        other = (z + NZ - k) % NZ
        return remote(z_out.at[z_lo], z_in.at[other], z_send.at[k], z_recv.at[k], at_z(other))

    for k in range(1, NZ):
        send_z(k).start()
    z_in[z] = z_out[z_lo]
    for k in range(1, NZ):
        take_z(k).wait_recv()
    result[1:2, :] = sum(z_in[k] for k in range(NZ))

    for k in range(1, NY):
        send_ext(k).wait_send()

    @pl.loop(0, GROUPS)
    def _(g):
        for k in range(1, NY):
            send_item(k, g).wait_send()
        send_near(g).wait_send()
        send_sibling(2 * g).wait_send()
        send_sibling(2 * g + 1).wait_send()

    for k in range(GROUPS // 2):
        send_mirror(k).wait_send()
        for j in range(1, NX):
            send_x(j, k).wait_send()
    for k in range(1, NY):
        send_part(k).wait_send()

    for k in range(1, 2 * NX):
        send_xc(k).wait_send()
    for k in range(1, NZ):
        send_z(k).wait_send()


def finish(result, loglik_out, tilt_out):
    loglik_out[...] = result[0, :ITEMS]
    for at in range(3):
        tilt_out[at] = result[1:2, at * TILTS : (at + 1) * TILTS]


def solution(mesh):
    placed = (
        P(("species", "series"), None),
        P(("species", "series")),
        P(None, ("species", "series")),
        P(("species", "series"), None),
        P(("species", "series"), None),
        P("species", None),
        P(("species", "series")),
        P(("species", "series")),
    )
    table, slopes = phase_tables()
    rows = frequency_rows()
    any_space = pl.BlockSpec(memory_space=pl.ANY)
    vmem = pl.BlockSpec(memory_space=pltpu.VMEM)
    smem = pl.BlockSpec(memory_space=pltpu.SMEM)
    dma = pltpu.SemaphoreType.DMA

    def body(observed, defocus, shift_center, pose_index, pose_logprior, reference_tiles, series_id, tilt_id):
        result = pl.pallas_call(
            kernel,
            out_shape=jax.ShapeDtypeStruct((8, LANES), F32),
            in_specs=[any_space, any_space, any_space, any_space, vmem, vmem, vmem, smem, smem, smem, smem],
            out_specs=vmem,
            scratch_shapes=[
                pltpu.VMEM((ITEMS, 2 * FREQ), BF16),
                pltpu.VMEM((GROUPS, 4, 2, 2 * POSES_SP, WIDTH), BF16),
                pltpu.VMEM((GROUPS, NY, 2, ITEMS, WIDTH), BF16),
                pltpu.VMEM((BLOCKS, 2, DEPTH, 2 * LANES), BF16),
                pltpu.VMEM((BLOCKS, 2 * DEPTH, LANES), BF16),
                pltpu.VMEM((NY, 2 * ITEMS, LANES), F32),
                pltpu.VMEM((NY, ITEMS, LANES), F32),
                pltpu.VMEM((2, NY, PAIRS * ITEMS, 4 * POSES_SP), BF16),
                pltpu.VMEM((2, NY, ITEMS, FREQ), BF16),
                pltpu.VMEM((2, ROWS, DEPTH), BF16),
                pltpu.VMEM((ROWS, 2 * DEPTH), BF16),
                pltpu.VMEM((2, 2, ROWS, 2 * LANES), F32),
                pltpu.VMEM((2, ROWS, LANES), F32),
                pltpu.VMEM((ITEMS, LANES), F32),
                pltpu.VMEM((NY, ITEMS, LANES), F32),
                pltpu.VMEM((NY, ITEMS, LANES), F32),
                pltpu.VMEM((NX, 8, LANES), F32),
                pltpu.VMEM((2 * NX, 8, LANES), F32),
                pltpu.VMEM((4, 1, LANES), F32),
                pltpu.VMEM((NZ, 1, LANES), F32),
                dma((2 * GROUPS + 1,)),
                dma((2 * BLOCKS,)),
                dma((NY, GROUPS)),
                dma((NY, GROUPS)),
                dma((GROUPS,)),
                dma((GROUPS,)),
                dma((NX, GROUPS // 2)),
                dma((2 * GROUPS,)),
                dma((2 * GROUPS,)),
                dma((2 * GROUPS,)),
                dma((NY,)),
                dma((NY,)),
                dma((NY,)),
                dma((NY,)),
                dma((2 * NX,)),
                dma((2 * NX,)),
                dma((NZ,)),
                dma((NZ,)),
            ],
            compiler_params=pltpu.CompilerParams(
                collective_id=0, has_side_effects=True, vmem_limit_bytes=60 * 2**20
            ),
        )(
            observed,
            reference_tiles,
            jnp.asarray(table),
            jnp.asarray(slopes),
            jnp.asarray(rows),
            pose_index,
            pose_logprior,
            defocus,
            shift_center,
            series_id,
            tilt_id,
        )
        return pl.pallas_call(
            finish,
            out_shape=(jax.ShapeDtypeStruct((ITEMS,), F32), jax.ShapeDtypeStruct((3, 1, TILTS), F32)),
            in_specs=[vmem],
            out_specs=(vmem, vmem),
        )(result)

    return jax.shard_map(
        body,
        mesh=mesh,
        in_specs=placed,
        out_specs=(P(("species", "series")), P(None, "series", None)),
        check_vma=False,
    )
```

```python
import functools
import math

import jax
import jax.numpy as jnp
import ml_dtypes
import numpy as np
from jax import lax
from jax.experimental import pallas as pl
from jax.experimental.pallas import tpu as pltpu
from jax.sharding import PartitionSpec as P

MESH = pl.DeviceIdType.MESH
F32 = jnp.float32
BF16 = jnp.bfloat16

BOX = 96
FREQ = 4608
SHIFT_Y = 8
SHIFT_X = 16
POSES_SP = 16
TILTS = 40
SCORE_SCALE = 0.03125
CTF_RATE = 4.0
AMP_PHASE = 0.1
ENV_RATE = 0.5
TWO_PI = 6.283185307179586

GROUPS = 6
WIDTH = FREQ // GROUPS
BLOCKS = GROUPS // 2
DEPTH = 2 * WIDTH
SUB = 256
LANES = 128
ITEMS = 16
NY = 4
NX = 4
NZ = 8
UNIT = WIDTH // 2
PAIRS = 8
ROWS = NY * PAIRS * ITEMS


def shift_halves():
    window = [(i - SHIFT_Y // 2, j - SHIFT_X // 2) for i in range(SHIFT_Y) for j in range(SHIFT_X)]
    inside = set(window)
    both = [s for s in window if s > (0, 0) and (-s[0], -s[1]) in inside]
    alone = [(0, 0)] + [s for s in window if (-s[0], -s[1]) not in inside]
    return both, alone


BOTH, ALONE = shift_halves()
N_BOTH, N_HALF = len(BOTH), len(BOTH) + len(ALONE)


def sine_fit():
    turn = np.cos(np.pi * (np.arange(400) + 0.5) / 400) * 0.5
    square = turn * turn
    odd = np.stack([turn * square**k for k in range(6)], 1)
    even = np.stack([square**k for k in range(7)], 1)
    sine = np.linalg.lstsq(odd, np.sin(2 * np.pi * turn), rcond=None)[0]
    cosine = np.linalg.lstsq(even, np.cos(2 * np.pi * turn), rcond=None)[0]
    return [float(np.float32(c)) for c in sine], [float(np.float32(c)) for c in cosine]


SINE, COSINE = sine_fit()


def sin_cos(turns):
    turn = turns - jnp.floor(turns + 0.5)
    square = turn * turn
    sine = SINE[-1]
    for c in SINE[-2::-1]:
        sine = sine * square + c
    cosine = COSINE[-1]
    for c in COSINE[-2::-1]:
        cosine = cosine * square + c
    return sine * turn, cosine


def frequencies():
    flat = np.arange(FREQ)
    row, col = flat // (BOX // 2), flat % (BOX // 2)
    return np.where(row < BOX // 2, row, row - BOX).astype(np.float64), col.astype(np.float64)


def frequency_rows():
    freq_y, freq_x = frequencies()
    k2 = (freq_y**2 + freq_x**2) / (BOX / 2.0) ** 2
    env = np.exp(-ENV_RATE * k2)
    rows = np.zeros((8, FREQ), np.float64)
    rows[0] = freq_y
    rows[1] = freq_x
    rows[2] = CTF_RATE * k2 / TWO_PI
    rows[3] = -env
    rows[4] = -CTF_RATE * k2 * env
    return rows.astype(np.float32)


def phase_tables():
    freq_y, freq_x = frequencies()
    half = np.array(BOTH + ALONE, np.float64)
    angle = TWO_PI / BOX * (freq_y[:, None] * half[None, :, 0] + freq_x[:, None] * half[None, :, 1])
    cosine, sine = np.cos(angle), np.sin(angle)
    rate_x, rate_y = (TWO_PI / BOX * freq_x)[:, None], (TWO_PI / BOX * freq_y)[:, None]
    table = np.zeros((2, FREQ, 2 * LANES), np.float64)
    slopes = np.zeros((2, FREQ, LANES), np.float64)
    for part, (value, slope) in enumerate(((cosine, -sine), (sine, cosine))):
        table[part, :, :N_HALF] = value
        table[part, :, N_HALF : N_HALF + N_BOTH] = rate_x * slope[:, :N_BOTH]
        table[part, :, LANES : LANES + N_HALF] = rate_y * slope
        table[part, :, LANES + N_HALF : LANES + 2 * N_HALF - N_BOTH] = rate_x * slope[:, N_BOTH:]
        slopes[part, :, :N_HALF] = value
        slopes[part, :, N_HALF:] = (1 - 2 * part) * value[:, :N_BOTH]
    table = table.reshape(2, BLOCKS, DEPTH, 2 * LANES).transpose(1, 0, 2, 3)
    slopes = slopes.reshape(2, BLOCKS, DEPTH, LANES).transpose(1, 0, 2, 3).reshape(BLOCKS, 2 * DEPTH, LANES)
    return [t.astype(np.float32).astype(ml_dtypes.bfloat16) for t in (table, slopes)]


def kernel(
    observed,
    reference_tiles,
    table_in,
    slopes_in,
    freq_rows,
    pose_index,
    pose_logprior,
    defocus,
    shift_center,
    series_id,
    tilt_id,
    result,
    raw,
    tiles,
    items,
    table,
    slopes,
    ext,
    priors,
    pose_hot,
    ctf,
    lhs,
    lhs_slope,
    acc,
    acc_slope,
    part_out,
    part_in,
    own_loglik,
    xc_out,
    xc_in,
    z_out,
    z_in,
    local_sem,
    table_sem,
    item_send,
    item_recv,
    near_send,
    near_recv,
    far_send,
    far_recv,
    sib_send,
    sib_recv,
    ext_send,
    ext_recv,
    part_send,
    part_recv,
    xc_send,
    xc_recv,
    z_send,
    z_recv,
):
    sp = lax.axis_index("species")
    se = lax.axis_index("series")
    z_hi, y, core = sp // 8, (sp // 2) % NY, sp % 2
    z_lo, x = se // NX, se % NX
    z, xc = z_hi * 4 + z_lo, x * 2 + core

    def at_y(other):
        return (z_hi * 8 + other * 2 + core, se)

    def at_z(other):
        return (other // 4 * 8 + y * 2 + core, other % 4 * NX + x)

    def at_xc(other):
        return (z_hi * 8 + y * 2 + other % 2, z_lo * NX + other // 2)

    sibling = (z_hi * 8 + y * 2 + 1 - core, se)
    mirror = at_z(NZ - 1 - z)
    own_tiles = z_hi * 2 + core
    own_far = (1 - z_hi) * 2 + core
    sibling_tiles = z_hi * 2 + 1 - core
    sibling_far = (1 - z_hi) * 2 + 1 - core

    barrier = pltpu.get_barrier_semaphore()
    partners = [at_y((y + k) % NY) for k in range(1, NY)]
    partners += [at_xc((xc + k) % (2 * NX)) for k in range(1, 2 * NX)]
    partners += [at_z((z + k) % NZ) for k in range(1, NZ)]
    for partner in partners:
        pl.semaphore_signal(barrier, inc=1, device_id=partner, device_id_type=MESH)

    raw_copy = pltpu.make_async_copy(observed, raw, local_sem.at[2 * GROUPS])
    raw_copy.start()

    def tile_copy(g, part):
        return pltpu.make_async_copy(
            reference_tiles.at[:, pl.ds(pl.multiple_of(part * FREQ + g * WIDTH, WIDTH), WIDTH)],
            tiles.at[g, own_tiles, part],
            local_sem.at[2 * g + part],
        )

    def table_copy(k):
        return pltpu.make_async_copy(table_in.at[k], table.at[k], table_sem.at[k])

    def slopes_copy(k):
        return pltpu.make_async_copy(slopes_in.at[k], slopes.at[k], table_sem.at[BLOCKS + k])

    @pl.loop(0, GROUPS)
    def _(g):
        tile_copy(g, 0).start()
        tile_copy(g, 1).start()

    def remote(src, dst, send, recv, device):
        return pltpu.make_async_remote_copy(
            src_ref=src, dst_ref=dst, send_sem=send, recv_sem=recv, device_id=device, device_id_type=MESH
        )

    def send_item(k, g):
        ref = items.at[g, y]
        return remote(ref, ref, item_send.at[k, g], item_recv.at[k, g], at_y((y + k) % NY))

    def take_item(k, g):
        other = (y + NY - k) % NY
        ref = items.at[g, other]
        return remote(ref, ref, item_send.at[k, g], item_recv.at[k, g], at_y(other))

    def send_near(g):
        ref = tiles.at[g, own_tiles]
        return remote(ref, ref, near_send.at[g], near_recv.at[g], sibling)

    def take_near(g):
        ref = tiles.at[g, sibling_tiles]
        return remote(ref, ref, near_send.at[g], near_recv.at[g], sibling)

    def unit(slot, u):
        return tiles.at[u // 2, slot, :, :, pl.ds(pl.multiple_of(u % 2 * UNIT, UNIT), UNIT)]

    def send_mirror(k):
        ref, u = unit(own_tiles, NX * k + x), NX * k + x
        return remote(ref, ref, far_send.at[0, k], far_recv.at[u], mirror)

    def send_x(j, k):
        ref, u = unit(own_far, NX * k + x), NX * k + x
        return remote(ref, ref, far_send.at[j, k], far_recv.at[u], (sp, z_lo * NX + (x + j) % NX))

    def take_far(j, k):
        u = NX * k + (x + j) % NX
        ref = unit(own_far, u)
        return remote(ref, ref, far_send.at[j, k], far_recv.at[u], mirror)

    def send_sibling(u):
        ref = unit(own_far, u)
        return remote(ref, ref, sib_send.at[u], sib_recv.at[u], sibling)

    def take_sibling(u):
        ref = unit(sibling_far, u)
        return remote(ref, ref, sib_send.at[u], sib_recv.at[u], sibling)

    def send_ext(k):
        ref = ext.at[y]
        return remote(ref, ref, ext_send.at[k], ext_recv.at[k], at_y((y + k) % NY))

    def take_ext(k):
        other = (y + NY - k) % NY
        ref = ext.at[other]
        return remote(ref, ref, ext_send.at[k], ext_recv.at[k], at_y(other))

    row16 = lax.broadcasted_iota(jnp.int32, (ITEMS, LANES), 0)
    lane16 = lax.broadcasted_iota(jnp.int32, (ITEMS, LANES), 1)

    def column(read):
        out = jnp.zeros((ITEMS, LANES), F32)
        for n in range(ITEMS):
            out = jnp.where(row16 == n, read(n).astype(F32), out)
        return out

    ext[y, :ITEMS, :] = jnp.concatenate([pose_index[...].astype(F32), pose_logprior[...]], 1)
    facts = jnp.where(lane16 == 0, column(lambda n: defocus[n]), column(lambda n: tilt_id[n]))
    ext[y, ITEMS:, :] = jnp.where(lane16 == 2, column(lambda n: series_id[n]), facts)

    center_y = column(lambda n: shift_center[0, n])
    center_x = column(lambda n: shift_center[1, n])
    center_y = jnp.concatenate([center_y, center_y], 1)
    center_x = jnp.concatenate([center_x, center_x], 1)
    pl.semaphore_wait(barrier, len(partners))

    for k in (2, 1, 3):
        send_ext(k).start()

    @pl.loop(0, GROUPS)
    def _(g):
        tile_copy(g, 0).wait()
        tile_copy(g, 1).wait()

        for half in range(2):

            @pl.when((2 * g + half) % NX == x)
            def _(half=half):
                send_mirror((2 * g + half) // NX).start()

    raw_copy.wait()

    @pl.loop(0, GROUPS)
    def _(g):
        for sub in range(WIDTH // SUB):
            at = g * WIDTH + sub * SUB
            re_cols = pl.ds(pl.multiple_of(at, SUB), SUB)
            im_cols = pl.ds(pl.multiple_of(FREQ + at, SUB), SUB)
            turns = freq_rows[0:1, re_cols] * center_y + freq_rows[1:2, re_cols] * center_x
            sine, cosine = sin_cos(turns * (1.0 / BOX))
            re, im = raw[:, re_cols].astype(F32), raw[:, im_cols].astype(F32)
            cols = slice(sub * SUB, (sub + 1) * SUB)
            items[g, y, 0, :, cols] = (re * cosine + im * sine).astype(BF16)
            items[g, y, 1, :, cols] = (im * cosine - re * sine).astype(BF16)
        for k in (2, 1, 3):
            send_item(k, g).start()
        send_near(g).start()

    for k in range(BLOCKS):
        table_copy(k).start()
        slopes_copy(k).start()
    acc[...] = jnp.zeros_like(acc)
    acc_slope[...] = jnp.zeros_like(acc_slope)

    lane_f = lane16.astype(F32)
    to_front = (LANES - 8 * y) % LANES

    @pl.loop(0, NY)
    def _(k):
        @pl.when(k > 0)
        def _():
            take_ext(k).wait_recv()

        b = (y + NY - k) % NY
        moved = pltpu.roll(ext[b, :ITEMS, :], to_front, 1)
        priors[b] = moved
        for h in range(2):
            for j in range(PAIRS):
                pose = moved[:, 32 * h + j : 32 * h + j + 1] + float((j // 2) * POSES_SP)
                hot = jnp.where(lane_f == pose, 1.0, 0.0)[:, : 4 * POSES_SP]
                pose_hot[h, b, j * ITEMS : (j + 1) * ITEMS, :] = hot.astype(BF16)
        focus = ext[b, ITEMS:, 0:1] + jnp.zeros((ITEMS, WIDTH), F32)

        @pl.loop(0, GROUPS)
        def _(g):
            cols = pl.ds(pl.multiple_of(g * WIDTH, WIDTH), WIDTH)
            turns = focus * freq_rows[2:3, cols] - AMP_PHASE / TWO_PI
            sine, cosine = sin_cos(turns)
            ctf[0, b, :, cols] = (sine * freq_rows[3:4, cols]).astype(BF16)
            ctf[1, b, :, cols] = (cosine * freq_rows[4:5, cols]).astype(BF16)

    def pass_own(k):
        take_far(0, k).wait_recv()
        for j in (2, 1, 3):
            send_x(j, k).start()
        send_sibling(NX * k + x).start()

    def pass_other(k):
        for j in range(1, NX):
            take_far(j, k).wait_recv()
            send_sibling(NX * k + (x + j) % NX).start()

    def fill(g, h, part):
        for sub in range(WIDTH // SUB):
            cols = slice(sub * SUB, (sub + 1) * SUB)
            tile_re = tiles[g, pl.ds(2 * h, 2), 0, :, cols].reshape(4 * POSES_SP, SUB)
            tile_im = tiles[g, pl.ds(2 * h, 2), 1, :, cols].reshape(4 * POSES_SP, SUB)
            freqs = pl.ds(pl.multiple_of(g * WIDTH + sub * SUB, SUB), SUB)
            at = part * WIDTH + sub * SUB
            for b in range(NY):
                hot = pose_hot[h, b]
                re = jnp.dot(hot, tile_re, preferred_element_type=F32).reshape(PAIRS, ITEMS, SUB).astype(BF16)
                im = jnp.dot(hot, tile_im, preferred_element_type=F32).reshape(PAIRS, ITEMS, SUB).astype(BF16)
                value, slope = ctf[0, b, :, freqs], ctf[1, b, :, freqs]
                o_re, o_im = items[g, b, 0, :, cols], items[g, b, 1, :, cols]
                prod_re = re * o_re + im * o_im
                prod_im = re * o_im - im * o_re
                rows = slice(b * PAIRS * ITEMS, (b + 1) * PAIRS * ITEMS)
                lhs[0, rows, at : at + SUB] = (prod_re * value).reshape(PAIRS * ITEMS, SUB)
                lhs[1, rows, at : at + SUB] = (prod_im * value).reshape(PAIRS * ITEMS, SUB)
                lhs_slope[rows, at : at + SUB] = (prod_re * slope).reshape(PAIRS * ITEMS, SUB)
                lhs_slope[rows, DEPTH + at : DEPTH + at + SUB] = (prod_im * slope).reshape(PAIRS * ITEMS, SUB)

    passing = ((0, 0, 0, True), (0, 1, 1, True), (1, 0, 2, True), (1, 1, 0, False), (2, 0, 1, False), (2, 1, 2, False))

    @pl.loop(0, 2 * BLOCKS)
    def _(i):
        far = jnp.where(i < 2, 0, jnp.where(i == 3, 0, 1))
        block = jnp.where(i < 2, i, jnp.where(i == 2, 0, jnp.where(i == 3, 2, i - 3)))
        h = (z_hi + far) % 2
        for part in range(2):
            g = 2 * block + part

            @pl.when(far == 0)
            def _(g=g):
                for k in range(1, NY):
                    take_item(k, g).wait_recv()
                take_near(g).wait_recv()

            @pl.when(far == 1)
            def _(g=g):
                take_sibling(2 * g).wait_recv()
                take_sibling(2 * g + 1).wait_recv()

            fill(g, h, part)
            for at, at_part, k, own in passing:
                if at_part == part:

                    @pl.when(i == at)
                    def _(k=k, own=own):
                        if own:
                            pass_own(k)
                        else:
                            pass_other(k)

        @pl.when(far == 0)
        def _():
            table_copy(block).wait()
            slopes_copy(block).wait()

        for q in range(2):
            acc[h, q] += jnp.dot(lhs[q], table[block, q], preferred_element_type=F32)
        acc_slope[h] += jnp.dot(lhs_slope[...], slopes[block], preferred_element_type=F32)

    plus_ok, minus_ok = lane16 < N_HALF, lane16 < N_BOTH
    lowest = -1e30
    part_out[...] = jnp.zeros_like(part_out)

    @pl.loop(0, NY)
    def _(b):
        message = priors[b]
        places = []
        for h in range(2):
            for j in range(PAIRS):
                places.append((h, j, pl.ds(pl.multiple_of((b * PAIRS + j) * ITEMS, ITEMS), ITEMS)))
        scores = []
        for h, j, rows in places:
            prior = message[:, 64 + 32 * h + j : 64 + 32 * h + j + 1]
            re, im = acc[h, 0, rows, :LANES], acc[h, 1, rows, :LANES]
            scores.append(
                (
                    jnp.where(plus_ok, SCORE_SCALE * (re + im) + prior, lowest),
                    jnp.where(minus_ok, SCORE_SCALE * (re - im) + prior, lowest),
                )
            )
        top = functools.reduce(jnp.maximum, [jnp.maximum(p, m) for p, m in scores])
        top = jnp.max(top, axis=1, keepdims=True)
        zero = jnp.zeros((ITEMS, LANES), F32)
        total, d_focus, d_x, d_x_alone, d_y = zero, zero, zero, zero, zero
        for (h, j, rows), (p, m) in zip(places, scores):
            p, m = jnp.exp(p - top), jnp.exp(m - top)
            total += p + m
            m_moved = pltpu.roll(m, N_HALF, 1)
            d_focus += (p + m_moved) * acc_slope[h, rows, :]
            re, im = acc[h, 0, rows, :LANES], acc[h, 1, rows, :LANES]
            d_x += pltpu.roll(p, N_HALF, 1) * (re + im) - m_moved * (re - im)
            re, im = acc[h, 0, rows, LANES:], acc[h, 1, rows, LANES:]
            d_y += p * (re + im) - m * (re - im)
            d_x_alone += pltpu.roll(p, N_HALF - N_BOTH, 1) * (re + im)
        d_x = jnp.where(lane16 >= N_HALF, d_x, 0.0)
        d_x += jnp.where((lane16 >= N_HALF) & (lane16 < 2 * N_HALF - N_BOTH), d_x_alone, 0.0)
        out = jnp.where(lane16 == 8 * b, top, part_out[...])
        for at, term in enumerate((total, d_focus, d_x, d_y)):
            out = jnp.where(lane16 == 8 * b + at + 1, jnp.sum(term, axis=1, keepdims=True), out)
        part_out[...] = out

    def send_part(k):
        other = (y + k) % NY
        return remote(part_out, part_in.at[y], part_send.at[k], part_recv.at[k], at_y(other))

    def take_part(k):
        other = (y + NY - k) % NY
        return remote(part_out, part_in.at[other], part_send.at[k], part_recv.at[k], at_y(other))

    for k in range(1, NY):
        send_part(k).start()
    part_in[y] = part_out[...]

    tilt, series = [], []
    for b in range(NY):
        tilt.append(ext[b, ITEMS:, 1:2] + jnp.zeros((ITEMS, LANES), F32))
        series.append(ext[b, ITEMS:, 2:3] + jnp.zeros((ITEMS, LANES), F32))
    for k in range(1, NY):
        take_part(k).wait_recv()

    placed = []
    for b in range(NY):
        parts = [part_in[src] for src in range(NY)]
        at_b = 8 * b
        tops = [part[:, at_b : at_b + 1] for part in parts]
        top = functools.reduce(jnp.maximum, tops)
        sums = sum(part * jnp.exp(t - top) for part, t in zip(parts, tops))
        total = sums[:, at_b + 1 : at_b + 2]
        grads = sums * SCORE_SCALE / total
        spread = jnp.zeros((ITEMS, LANES), F32)
        for at in range(3):
            spread = jnp.where(lane_f == tilt[b] + float(at * TILTS), grads[:, at_b + 2 + at : at_b + 3 + at], spread)
        placed.append(spread)
        own_loglik[b] = top + jnp.log(total) + jnp.zeros((ITEMS, LANES), F32)
    row8 = lax.broadcasted_iota(jnp.int32, (8, LANES), 0)
    for to in range(NX):
        rows = jnp.zeros((8, LANES), F32)
        for lo in range(4):
            hits = [jnp.where(s == float(lo * NX + to), p, 0.0) for s, p in zip(series, placed)]
            rows = jnp.where(row8 == lo, jnp.sum(sum(hits), axis=0, keepdims=True), rows)
        xc_out[to] = rows

    def send_xc(k):
        other = (xc + k) % (2 * NX)
        return remote(xc_out.at[other // 2], xc_in.at[xc], xc_send.at[k], xc_recv.at[k], at_xc(other))

    def take_xc(k):
        other = (xc + 2 * NX - k) % (2 * NX)
        return remote(xc_out.at[x], xc_in.at[other], xc_send.at[k], xc_recv.at[k], at_xc(other))

    for k in range(1, 2 * NX):
        send_xc(k).start()
    xc_in[xc] = xc_out[x]
    loglik = own_loglik[y]
    result[0:1, :] = jnp.sum(jnp.where(row16 == lane16, loglik, 0.0), axis=0, keepdims=True)
    for k in range(1, 2 * NX):
        take_xc(k).wait_recv()
    rows = sum(xc_in[k] for k in range(2 * NX))
    for lo in range(4):
        z_out[lo] = rows[lo : lo + 1]

    def send_z(k):
        other = (z + k) % NZ
        return remote(z_out.at[other % 4], z_in.at[z], z_send.at[k], z_recv.at[k], at_z(other))

    def take_z(k):
        other = (z + NZ - k) % NZ
        return remote(z_out.at[z_lo], z_in.at[other], z_send.at[k], z_recv.at[k], at_z(other))

    for k in range(1, NZ):
        send_z(k).start()
    z_in[z] = z_out[z_lo]
    for k in range(1, NZ):
        take_z(k).wait_recv()
    result[1:2, :] = sum(z_in[k] for k in range(NZ))

    for k in range(1, NY):
        send_ext(k).wait_send()

    @pl.loop(0, GROUPS)
    def _(g):
        for k in range(1, NY):
            send_item(k, g).wait_send()
        send_near(g).wait_send()
        send_sibling(2 * g).wait_send()
        send_sibling(2 * g + 1).wait_send()

    for k in range(GROUPS // 2):
        send_mirror(k).wait_send()
        for j in range(1, NX):
            send_x(j, k).wait_send()
    for k in range(1, NY):
        send_part(k).wait_send()

    for k in range(1, 2 * NX):
        send_xc(k).wait_send()
    for k in range(1, NZ):
        send_z(k).wait_send()


def finish(result, loglik_out, tilt_out):
    loglik_out[...] = result[0, :ITEMS]
    for at in range(3):
        tilt_out[at] = result[1:2, at * TILTS : (at + 1) * TILTS]


def solution(mesh):
    placed = (
        P(("species", "series"), None),
        P(("species", "series")),
        P(None, ("species", "series")),
        P(("species", "series"), None),
        P(("species", "series"), None),
        P("species", None),
        P(("species", "series")),
        P(("species", "series")),
    )
    table, slopes = phase_tables()
    rows = frequency_rows()
    any_space = pl.BlockSpec(memory_space=pl.ANY)
    vmem = pl.BlockSpec(memory_space=pltpu.VMEM)
    smem = pl.BlockSpec(memory_space=pltpu.SMEM)
    dma = pltpu.SemaphoreType.DMA

    def body(observed, defocus, shift_center, pose_index, pose_logprior, reference_tiles, series_id, tilt_id):
        result = pl.pallas_call(
            kernel,
            out_shape=jax.ShapeDtypeStruct((8, LANES), F32),
            in_specs=[any_space, any_space, any_space, any_space, vmem, vmem, vmem, smem, smem, smem, smem],
            out_specs=vmem,
            scratch_shapes=[
                pltpu.VMEM((ITEMS, 2 * FREQ), BF16),
                pltpu.VMEM((GROUPS, 4, 2, 2 * POSES_SP, WIDTH), BF16),
                pltpu.VMEM((GROUPS, NY, 2, ITEMS, WIDTH), BF16),
                pltpu.VMEM((BLOCKS, 2, DEPTH, 2 * LANES), BF16),
                pltpu.VMEM((BLOCKS, 2 * DEPTH, LANES), BF16),
                pltpu.VMEM((NY, 2 * ITEMS, LANES), F32),
                pltpu.VMEM((NY, ITEMS, LANES), F32),
                pltpu.VMEM((2, NY, PAIRS * ITEMS, 4 * POSES_SP), BF16),
                pltpu.VMEM((2, NY, ITEMS, FREQ), BF16),
                pltpu.VMEM((2, ROWS, DEPTH), BF16),
                pltpu.VMEM((ROWS, 2 * DEPTH), BF16),
                pltpu.VMEM((2, 2, ROWS, 2 * LANES), F32),
                pltpu.VMEM((2, ROWS, LANES), F32),
                pltpu.VMEM((ITEMS, LANES), F32),
                pltpu.VMEM((NY, ITEMS, LANES), F32),
                pltpu.VMEM((NY, ITEMS, LANES), F32),
                pltpu.VMEM((NX, 8, LANES), F32),
                pltpu.VMEM((2 * NX, 8, LANES), F32),
                pltpu.VMEM((4, 1, LANES), F32),
                pltpu.VMEM((NZ, 1, LANES), F32),
                dma((2 * GROUPS + 1,)),
                dma((2 * BLOCKS,)),
                dma((NY, GROUPS)),
                dma((NY, GROUPS)),
                dma((GROUPS,)),
                dma((GROUPS,)),
                dma((NX, GROUPS // 2)),
                dma((2 * GROUPS,)),
                dma((2 * GROUPS,)),
                dma((2 * GROUPS,)),
                dma((NY,)),
                dma((NY,)),
                dma((NY,)),
                dma((NY,)),
                dma((2 * NX,)),
                dma((2 * NX,)),
                dma((NZ,)),
                dma((NZ,)),
            ],
            compiler_params=pltpu.CompilerParams(
                collective_id=0, has_side_effects=True, vmem_limit_bytes=60 * 2**20
            ),
        )(
            observed,
            reference_tiles,
            jnp.asarray(table),
            jnp.asarray(slopes),
            jnp.asarray(rows),
            pose_index,
            pose_logprior,
            defocus,
            shift_center,
            series_id,
            tilt_id,
        )
        return pl.pallas_call(
            finish,
            out_shape=(jax.ShapeDtypeStruct((ITEMS,), F32), jax.ShapeDtypeStruct((3, 1, TILTS), F32)),
            in_specs=[vmem],
            out_specs=(vmem, vmem),
        )(result)

    return jax.shard_map(
        body,
        mesh=mesh,
        in_specs=placed,
        out_specs=(P(("species", "series")), P(None, "series", None)),
        check_vma=False,
    )
```
